1024 devices in a mesh: rep: 8 (over x, core), own: 32 (over z_lo, y), blk: 4 (over z_hi).
Axes of the slice: x: 4, y: 8, z: 16 (z_hi: 4, z_lo: 4; z = z_hi * 4 + z_lo), core: 2. Of those that a mesh axis runs over, the one named last changes fastest.
Arguments:
- partial_grads: bfloat16 [8, 64, 1024, 1024], P('rep', 'own', None, 'blk'), may hold values from -6 to 6
- owner_map: int32 [64], replicated, may hold values from 0 to 31, as said below
- iterations: int32 [64], replicated, may hold values from 1 to 2
- slot_history: bfloat16 [32, 4, 1024, 1024], P('own', 'blk'), may hold values from -0.02 to 0.5, as said below
Outputs:
- directions: bfloat16 [64, 1024, 1024], P('own', 'rep', 'blk')
- new_statistic: bfloat16 [32, 4, 1024, 1024], P('own', 'blk', 'rep')
The draws below stay inside these ranges and needn't reach their ends.
Inputs may be any that keep to these rules, and one draw needn't show every extreme that they name: `owner_map`: the 2 blocks of one home group name different owners; no owner is named by more than 4 blocks in all, and some owner by exactly 4. `slot_history`: each matrix is symmetric.
All inputs are finite; a program needn't handle non-finite values.
Results may differ from the reference program's by a relative error of at most 0.02.
Values may be sent and summed in bfloat16 or wider, within the bound.
No kernel may reach another device: no remote copies, remote signals or barrier semaphores. Data moves between devices by JAX's collectives and lax.ppermute only.
A program may use at most 64 MiB of HBM per device.

```python
import math
import jax
import jax.numpy as jnp
from jax import lax

B = 1024
ITERS = 2
NBO = 2
TOTAL = 64
N_REP = 8
N_OWN = 32
N_BLK = 4


def draw_owner_map(key, part):
    key = jax.random.fold_in(key, 5)
    key_owner, key_home, key_turn = jax.random.split(key, 3)
    count_all = N_OWN * NBO
    position = jnp.arange(count_all, dtype=jnp.int32)
    heavy_span = N_OWN // 4 * 2 * NBO
    canonical = jnp.where(position < heavy_span, position // (2 * NBO), N_OWN // 4 + (position - heavy_span) // NBO)
    labels = jax.random.permutation(key_owner, N_OWN).astype(jnp.int32)
    first_spot = jnp.argmax(jnp.where(labels == 0, 1, 0)).astype(jnp.int32)
    labels = labels.at[first_spot].set(labels[0]).at[0].set(0)
    light_spot = N_OWN // 4
    last_spot = jnp.argmax(jnp.where(labels == N_OWN - 1, 1, 0)).astype(jnp.int32)
    labels = labels.at[last_spot].set(labels[light_spot]).at[light_spot].set(N_OWN - 1)
    labelled = labels[canonical]
    grid_owner = labelled.reshape(NBO, N_OWN).T
    home_order = jax.random.permutation(key_home, N_OWN).astype(jnp.int32)
    grid_owner = grid_owner[home_order]
    turned = jax.random.randint(key_turn, (N_OWN, 1), 0, NBO).astype(jnp.int32)
    column_ids = (jnp.arange(NBO, dtype=jnp.int32)[None, :] + turned) % NBO
    grid_owner = jnp.take_along_axis(grid_owner, column_ids, axis=1)
    return grid_owner.reshape(-1).astype(jnp.int32)


def draw_slot_history(key, part):
    key = jax.random.fold_in(key, 9)
    key_diag, key_noise = jax.random.split(key, 2)
    diagonal = jnp.exp(jax.random.uniform(key_diag, (N_OWN, N_BLK, B), jnp.float32, math.log(0.05), math.log(0.5)))
    noise = jax.random.uniform(key_noise, (N_OWN, N_BLK, B, B), jnp.float32, -1.0, 1.0)
    symmetric = (noise + jnp.swapaxes(noise, 2, 3)) * (0.5 / B)
    identity = jnp.eye(B, dtype=jnp.float32)
    return (symmetric * (1.0 - identity) + diagonal[..., None] * identity).astype(jnp.bfloat16)


def plant(values, rng, smallest, largest):
    longest = values.shape.index(max(values.shape))
    spots = []
    for shift in (0, 1):
        where = [jax.random.randint(jax.random.fold_in(rng, axis), (), 0, length) for axis, length in enumerate(values.shape)]
        where[longest] = (where[longest] + shift) % values.shape[longest]
        spots.append(tuple(where))
    return values.at[spots[0]].set(smallest).at[spots[1]].set(largest)


def level_of(rng, dims, pieces, least, largest):
    loudness = 1.0
    for dim, shards_of in pieces:
        steps = jax.random.uniform(jax.random.fold_in(jax.random.fold_in(rng, 6), dim), (shards_of,), jnp.float32, least / len(pieces), largest / len(pieces))
        loudness = loudness * jnp.repeat(jnp.exp(steps), dims[dim] // shards_of).reshape((-1,) + (1,) * (len(dims) - 1 - dim))
    return loudness


def bell_draw(key, extent, spread, bound, cuts=(), kind=jnp.bfloat16):
    array = jax.random.normal(key, extent, jnp.float32) * spread
    if len(cuts) > 0:
        array = level_of(key, extent, cuts, -0.22, 0.18) * array
    return jnp.clip(array, min=-bound, max=bound).astype(kind)


def setup_inputs(seed: int = 0) -> dict:
    arg_keys = jax.random.split(jax.random.key(seed), 5)
    partial_grads = bell_draw(arg_keys[0], (N_REP, TOTAL, B, B), 0.4, 6.0, ((0, 8), (1, 32), (3, 4)))
    owner_map = draw_owner_map(jax.random.fold_in(arg_keys[4], 71), 0)
    iterations = plant(jax.random.randint(arg_keys[2], (TOTAL,), 1, ITERS + 1), jax.random.fold_in(arg_keys[2], 1), 1, ITERS).astype(jnp.int32)
    slot_history = draw_slot_history(jax.random.fold_in(arg_keys[4], 71), 0)
    return dict(partial_grads=partial_grads, owner_map=owner_map, iterations=iterations, slot_history=slot_history)


DECAY = 0.5
DAMPING = 0.05

def precondition(grad_block, history, iter_need):
    order_full = grad_block.shape[0]
    identity = jnp.eye(order_full, dtype=jnp.float32)
    gram = jnp.dot(grad_block, grad_block.T, preferred_element_type=jnp.float32)
    statistic = DECAY * history.astype(jnp.float32) + (1.0 - DECAY) * gram / order_full + DAMPING * identity
    frobenius = jnp.sqrt(jnp.sum(statistic * statistic))
    norm_scale = math.sqrt(order_full) / (2.0 * frobenius)
    scaled_half = (statistic * norm_scale).astype(jnp.bfloat16)
    factor = 1.5 * identity - 0.5 * scaled_half.astype(jnp.float32)
    factor_half = factor.astype(jnp.bfloat16)
    y_first = jnp.dot(scaled_half, factor_half, preferred_element_type=jnp.float32)
    product = jnp.dot(factor_half, y_first.astype(jnp.bfloat16), preferred_element_type=jnp.float32)
    update = 1.5 * identity - 0.5 * product
    z_second = jnp.dot(factor_half, update.astype(jnp.bfloat16), preferred_element_type=jnp.float32)
    root_block = jnp.where(iter_need >= ITERS, z_second, factor)
    raw_direction = jnp.dot(root_block.astype(jnp.bfloat16).T, grad_block, preferred_element_type=jnp.float32)
    return (raw_direction.astype(jnp.bfloat16), statistic.astype(jnp.bfloat16))

def reference(partial_grads, owner_map, iterations, slot_history):
    owner_ids = owner_map.astype(jnp.int32)
    position = jnp.arange(TOTAL, dtype=jnp.int32)
    same_owner = owner_ids[:, None] == owner_ids[None, :]
    earlier = position[None, :] < position[:, None]
    slot_index = lax.optimization_barrier(jnp.sum(jnp.where(same_owner & earlier, 1, 0), axis=1)).astype(jnp.int32)

    def one_block(block_index):
        partials = lax.dynamic_index_in_dim(partial_grads, block_index, 1, keepdims=False)
        grad_block = lax.optimization_barrier(jnp.sum(partials.astype(jnp.float32), axis=0)).astype(jnp.bfloat16)
        history = slot_history[owner_ids[block_index], slot_index[block_index]]
        return precondition(grad_block, history, iterations[block_index])
    directions, statistics = lax.map(one_block, position)
    new_statistic = slot_history.at[owner_ids, slot_index].set(statistics)
    return (directions, new_statistic)
```

```python
import functools
import math

import jax
import jax.numpy as jnp
from jax import lax
from jax.experimental import pallas as pl
from jax.experimental.pallas import tpu as pltpu
from jax.sharding import PartitionSpec as P

ITERS = 2


DECAY = 0.5
DAMPING = 0.05


def gram_kernel(place, mine, other, out):
    shards = mine.shape[0]
    home_count, band_rows = out.shape[0], out.shape[1]
    for block in range(home_count):
        parts = []
        for half in range(other.shape[0]):
            total = jnp.zeros((band_rows, band_rows), jnp.float32)
            for shard in range(shards):
                total = total + lax.dot_general(
                    mine[shard, block],
                    other[half, shard, block],
                    (((1,), (1,)), ((), ())),
                    preferred_element_type=jnp.float32,
                )
            parts.append(total)
        out[block] = jnp.concatenate(parts, axis=1)


def gram_tile(place, mine, gathered):
    replicas, shards, home_count, band_rows, band_cols = gathered.shape
    span = band_cols // band_rows
    return pl.pallas_call(
        gram_kernel,
        out_shape=jax.ShapeDtypeStruct((home_count, band_rows, band_cols), jnp.float32),
        grid_spec=pltpu.PrefetchScalarGridSpec(
            num_scalar_prefetch=1,
            grid=(1,),
            in_specs=[
                pl.BlockSpec(mine.shape, lambda i, place: (0, 0, 0, 0)),
                pl.BlockSpec(
                    (span, shards, home_count, band_rows, band_cols),
                    lambda i, place: (place[1], 0, 0, 0, 0),
                ),
            ],
            out_specs=pl.BlockSpec((home_count, band_rows, band_cols), lambda i, place: (0, 0, 0)),
        ),
        compiler_params=pltpu.CompilerParams(vmem_limit_bytes=32 * 1024 * 1024),
    )(place, mine, gathered)


def newton_kernel(place, need, stat, cols, out, scaled, factor):
    replicas, shards, _, band_rows, band_cols = stat.shape
    order_full = replicas * band_rows
    block = pl.program_id(0)
    squares = jnp.zeros((8, band_cols), jnp.float32)
    for band in range(replicas):
        for shard in range(shards):
            tile = stat[band, shard, 0].astype(jnp.float32)
            squares = squares + jnp.sum((tile * tile).reshape(-1, 8, band_cols), axis=0)
    frobenius = jnp.sqrt(jnp.sum(squares, keepdims=True)[:1, :1])
    norm_scale = math.sqrt(order_full) / (2.0 * frobenius)
    row_ids = lax.broadcasted_iota(jnp.int32, (band_rows, band_cols), 0)
    col_ids = lax.broadcasted_iota(jnp.int32, (band_rows, band_cols), 1)
    for band in range(replicas):
        for shard in range(shards):
            tile = (stat[band, shard, 0].astype(jnp.float32) * norm_scale).astype(jnp.bfloat16)
            rows, columns = pl.ds(band * band_rows, band_rows), pl.ds(shard * band_cols, band_cols)
            scaled[rows, columns] = tile
            rest = -0.5 * tile.astype(jnp.float32)
            if (band * band_rows) // band_cols == shard:
                diagonal = row_ids + (band * band_rows - shard * band_cols) == col_ids
                rest = rest + jnp.where(diagonal, 1.5, 0.0)
            factor[rows, columns] = rest.astype(jnp.bfloat16)
    first = pl.multiple_of(place[0] * band_rows, band_rows)
    mine = factor[pl.ds(first, band_rows), :]
    product = jnp.dot(mine, scaled[...], preferred_element_type=jnp.float32).astype(jnp.bfloat16)
    product = jnp.dot(product, factor[...], preferred_element_type=jnp.float32)
    wide_rows = lax.broadcasted_iota(jnp.int32, (band_rows, order_full), 0) + first
    wide_cols = lax.broadcasted_iota(jnp.int32, (band_rows, order_full), 1)
    update = jnp.where(wide_rows == wide_cols, 1.5, 0.0) - 0.5 * product
    second = jnp.dot(update.astype(jnp.bfloat16), factor[...], preferred_element_type=jnp.float32)
    root = jnp.where(need[block] >= ITERS, second, mine.astype(jnp.float32)).astype(jnp.bfloat16)
    total = jnp.zeros((band_rows, band_cols), jnp.float32)
    for band in range(replicas):
        total = total + jnp.dot(
            root[:, band * band_rows : (band + 1) * band_rows],
            cols[band, 0, 0],
            preferred_element_type=jnp.float32,
        )
    out[0] = total.astype(jnp.bfloat16)


def newton_tile(place, need, stat, gathered):
    replicas, shards, home_count, band_rows, band_cols = stat.shape
    order_full = replicas * band_rows
    return pl.pallas_call(
        newton_kernel,
        out_shape=jax.ShapeDtypeStruct((home_count, band_rows, band_cols), jnp.bfloat16),
        grid_spec=pltpu.PrefetchScalarGridSpec(
            num_scalar_prefetch=2,
            grid=(home_count,),
            in_specs=[
                pl.BlockSpec(
                    (replicas, shards, 1, band_rows, band_cols),
                    lambda i, place, need: (0, 0, i, 0, 0),
                ),
                pl.BlockSpec(
                    (replicas, 1, 1, band_rows, band_cols),
                    lambda i, place, need: (0, place[1], i, 0, 0),
                ),
            ],
            out_specs=pl.BlockSpec((1, band_rows, band_cols), lambda i, place, need: (i, 0, 0)),
            scratch_shapes=[
                pltpu.VMEM((order_full, order_full), jnp.bfloat16),
                pltpu.VMEM((order_full, order_full), jnp.bfloat16),
            ],
        ),
        compiler_params=pltpu.CompilerParams(vmem_limit_bytes=40 * 1024 * 1024),
    )(place, need, stat, gathered)


def exchange(array, axis):
    return lax.all_to_all(array, axis, split_axis=0, concat_axis=0, tiled=True)


def spread(tiles, targets, count):
    ids = lax.broadcasted_iota(jnp.int32, (count, 1, 1), 0)
    out = jnp.zeros((count,) + tiles.shape[1:], tiles.dtype)
    for index in range(tiles.shape[0]):
        out = jnp.where(ids == targets[index], tiles[index][None], out)
    return out


def pick(tiles, index):
    return lax.dynamic_index_in_dim(tiles, index, 0, keepdims=False)


def body(partial_grads, owner_map, iterations, slot_history):
    owners = lax.axis_size("own")
    replicas = lax.axis_size("rep")
    shards = lax.axis_size("blk")
    my_rep, my_own, my_blk = lax.axis_index("rep"), lax.axis_index("own"), lax.axis_index("blk")
    _, home_count, order_full, band_cols = partial_grads.shape
    band_rows = order_full // replicas
    total_blocks = owner_map.shape[0]
    history = slot_history[0, 0]

    outgoing = (
        partial_grads[0]
        .reshape(home_count, replicas, band_rows, band_cols)
        .transpose(1, 0, 2, 3)
    )
    partials = exchange(outgoing, "rep")
    grad_tile = jnp.sum(partials.astype(jnp.float32), axis=0).astype(jnp.bfloat16)

    grad_band = lax.all_gather(grad_tile, "blk", axis=0, tiled=False)
    grad_full = lax.all_gather(grad_band, "rep", axis=0, tiled=False)

    position = jnp.arange(total_blocks, dtype=jnp.int32)
    same = owner_map[:, None] == owner_map[None, :]
    slot = jnp.sum(jnp.where(same & (position[None, :] < position[:, None]), 1, 0), axis=1)
    slot_ids = jnp.arange(shards, dtype=jnp.int32)
    held = (owner_map[None, :] == my_own) & (slot[None, :] == slot_ids[:, None])
    holder = jnp.sum(jnp.where(held, position[None, :] + 1, 0), axis=1)
    home_of = jnp.where(holder > 0, (holder - 1) // home_count, -1)
    my_owners = lax.dynamic_slice_in_dim(owner_map, my_own * home_count, home_count)
    my_need = lax.dynamic_slice_in_dim(iterations, my_own * home_count, home_count)

    history_rows = lax.dynamic_slice_in_dim(history, my_rep * band_rows, band_rows, 0)
    history_rows, _ = lax.optimization_barrier((history_rows, grad_tile))
    history_parts = history_rows.reshape(band_rows, shards, band_cols).transpose(1, 0, 2)
    history_tiles = exchange(history_parts, "blk")
    history_sent = spread(history_tiles, home_of, owners)
    history_came = exchange(history_sent, "own")
    history_mine = jnp.stack([pick(history_came, my_owners[i]) for i in range(home_count)])

    place = jnp.stack([my_rep, my_blk]).astype(jnp.int32)
    gram = gram_tile(place, grad_band, grad_full) * ((1.0 - DECAY) / order_full)
    row_ids = my_rep * band_rows + lax.broadcasted_iota(jnp.int32, (band_rows, band_cols), 0)
    col_ids = my_blk * band_cols + lax.broadcasted_iota(jnp.int32, (band_rows, band_cols), 1)
    damping = jnp.where(row_ids == col_ids, DAMPING, 0.0)
    stat_tile = (DECAY * history_mine.astype(jnp.float32) + gram + damping).astype(jnp.bfloat16)

    stat_band = lax.all_gather(stat_tile, "blk", axis=0, tiled=False)
    stat_full = lax.all_gather(stat_band, "rep", axis=0, tiled=False)

    gram_sent = spread(gram.astype(jnp.bfloat16), my_owners, owners)
    gram_came = exchange(gram_sent, "own")
    gram_slots = jnp.stack([pick(gram_came, jnp.maximum(home_of[i], 0)) for i in range(shards)])
    gram_rows = exchange(gram_slots, "blk").transpose(1, 0, 2).reshape(band_rows, order_full)
    own_rows = lax.dynamic_slice_in_dim(history, my_rep * band_rows, band_rows, 0)
    wide_rows = my_rep * band_rows + lax.broadcasted_iota(jnp.int32, (band_rows, order_full), 0)
    wide_cols = lax.broadcasted_iota(jnp.int32, (band_rows, order_full), 1)
    fresh = (
        DECAY * own_rows.astype(jnp.float32)
        + gram_rows.astype(jnp.float32)
        + jnp.where(wide_rows == wide_cols, DAMPING, 0.0)
    ).astype(jnp.bfloat16)
    occupied = lax.dynamic_index_in_dim(holder, my_blk, 0, keepdims=False) > 0
    new_rows = jnp.where(occupied, fresh, own_rows)

    directions = newton_tile(place, my_need, stat_full, grad_full)
    return (directions, new_rows[None, None])


def solution(mesh):
    return jax.shard_map(
        body,
        mesh=mesh,
        in_specs=(P("rep", "own", None, "blk"), P(), P(), P("own", "blk", None, None)),
        out_specs=(P("own", "rep", "blk"), P("own", "blk", "rep", None)),
        check_vma=False,
    )
```

```python
import functools
import math

import jax
import jax.numpy as jnp
from jax import lax
from jax.experimental import pallas as pl
from jax.experimental.pallas import tpu as pltpu
from jax.sharding import Mesh, PartitionSpec as P

ITERS = 2


DECAY = 0.5
DAMPING = 0.05

REP = ("x", "core")
OWN = ("zl", "y")
BLK = "zh"
RING = ("zl", "zh")
BIG = pltpu.CompilerParams(vmem_limit_bytes=40 * 1024 * 1024)


def take_kernel(index, tiles, out):
    for place in range(out.shape[0]):
        out[place] = tiles[index[place]]


def take(tiles, index):
    return pl.pallas_call(
        take_kernel,
        out_shape=jax.ShapeDtypeStruct((index.shape[0],) + tiles.shape[1:], tiles.dtype),
        in_specs=[
            pl.BlockSpec(memory_space=pltpu.SMEM),
            pl.BlockSpec(memory_space=pltpu.VMEM),
        ],
        out_specs=pl.BlockSpec(memory_space=pltpu.VMEM),
        compiler_params=BIG,
    )(index, tiles)


def cut_kernel(place, rows, out):
    width = out.shape[2]
    for shard in range(out.shape[0]):
        out[shard] = rows[:, shard * width : (shard + 1) * width]


def cut_rows(place, history, shards, band_rows):
    order_full = history.shape[1]
    shape = (shards, band_rows, order_full // shards)
    return pl.pallas_call(
        cut_kernel,
        out_shape=jax.ShapeDtypeStruct(shape, history.dtype),
        grid_spec=pltpu.PrefetchScalarGridSpec(
            num_scalar_prefetch=1,
            grid=(1,),
            in_specs=[pl.BlockSpec((band_rows, order_full), lambda i, place: (place[0], 0))],
            out_specs=pl.BlockSpec(shape, lambda i, place: (0, 0, 0)),
        ),
        compiler_params=BIG,
    )(place, history)


def gram_kernel(place, mine, other, out, half_out):
    shards = mine.shape[0]
    home_count, band_rows = out.shape[0], out.shape[1]
    order_full = shards * out.shape[2]
    for block in range(home_count):
        for half in range(other.shape[0]):
            total = jnp.zeros((band_rows, band_rows), jnp.float32)
            for shard in range(shards):
                total = total + lax.dot_general(
                    mine[shard, block],
                    other[half, shard, block],
                    (((1,), (1,)), ((), ())),
                    preferred_element_type=jnp.float32,
                )
            total = total * ((1.0 - DECAY) / order_full)
            columns = slice(half * band_rows, (half + 1) * band_rows)
            out[block, :, columns] = total
            half_out[block, :, columns] = total.astype(jnp.bfloat16)


def gram_tile(place, mine, gathered):
    replicas, shards, home_count, band_rows, band_cols = gathered.shape
    span = band_cols // band_rows
    shape = (home_count, band_rows, band_cols)
    return pl.pallas_call(
        gram_kernel,
        out_shape=(
            jax.ShapeDtypeStruct(shape, jnp.float32),
            jax.ShapeDtypeStruct(shape, jnp.bfloat16),
        ),
        grid_spec=pltpu.PrefetchScalarGridSpec(
            num_scalar_prefetch=1,
            grid=(1,),
            in_specs=[
                pl.BlockSpec(mine.shape, lambda i, place: (0, 0, 0, 0)),
                pl.BlockSpec(
                    (span, shards, home_count, band_rows, band_cols),
                    lambda i, place: (place[1], 0, 0, 0, 0),
                ),
            ],
            out_specs=[pl.BlockSpec(shape, lambda i, place: (0, 0, 0))] * 2,
        ),
        compiler_params=BIG,
    )(place, mine, gathered)


def stat_kernel(place, owners, gram, came, out):
    home_count, band_rows, band_cols = out.shape
    row_ids = place[0] * band_rows + lax.broadcasted_iota(jnp.int32, (band_rows, band_cols), 0)
    col_ids = place[1] * band_cols + lax.broadcasted_iota(jnp.int32, (band_rows, band_cols), 1)
    damping = jnp.where(row_ids == col_ids, DAMPING, 0.0)
    for block in range(home_count):
        history = came[owners[block]].astype(jnp.float32)
        out[block] = (DECAY * history + gram[block] + damping).astype(jnp.bfloat16)


def stat_tile(place, owners, gram, came):
    return pl.pallas_call(
        stat_kernel,
        out_shape=jax.ShapeDtypeStruct(gram.shape, jnp.bfloat16),
        in_specs=[pl.BlockSpec(memory_space=pltpu.SMEM)] * 2
        + [pl.BlockSpec(memory_space=pltpu.VMEM)] * 2,
        out_specs=pl.BlockSpec(memory_space=pltpu.VMEM),
        compiler_params=BIG,
    )(place, owners, gram, came)


def fresh_kernel(place, rows, gram, out):
    shards, band_rows, band_cols = gram.shape
    row_ids = place[0] * band_rows + lax.broadcasted_iota(jnp.int32, (band_rows, band_cols), 0)
    col_ids = lax.broadcasted_iota(jnp.int32, (band_rows, band_cols), 1)
    for shard in range(shards):
        columns = slice(shard * band_cols, (shard + 1) * band_cols)
        history = rows[:, columns].astype(jnp.float32)
        came = gram[lax.rem(shard + place[1], shards)].astype(jnp.float32)
        damping = jnp.where(row_ids == col_ids + shard * band_cols, DAMPING, 0.0)
        fresh = DECAY * history + came + damping
        out[:, columns] = jnp.where(place[2] > 0, fresh, history).astype(jnp.bfloat16)


def fresh_rows(place, history, gram):
    shards, band_rows, _ = gram.shape
    order_full = history.shape[1]
    return pl.pallas_call(
        fresh_kernel,
        out_shape=jax.ShapeDtypeStruct((band_rows, order_full), jnp.bfloat16),
        grid_spec=pltpu.PrefetchScalarGridSpec(
            num_scalar_prefetch=1,
            grid=(1,),
            in_specs=[
                pl.BlockSpec((band_rows, order_full), lambda i, place: (place[0], 0)),
                pl.BlockSpec(gram.shape, lambda i, place: (0, 0, 0)),
            ],
            out_specs=pl.BlockSpec((band_rows, order_full), lambda i, place: (0, 0)),
        ),
        compiler_params=BIG,
    )(place, history, gram)


def newton_kernel(place, need, stat, cols, out, scaled, factor):
    replicas, shards, _, band_rows, band_cols = stat.shape
    order_full = replicas * band_rows
    block = pl.program_id(0)
    squares = jnp.zeros((8, band_cols), jnp.float32)
    for band in range(replicas):
        for shard in range(shards):
            tile = stat[band, shard, 0].astype(jnp.float32)
            squares = squares + jnp.sum((tile * tile).reshape(-1, 8, band_cols), axis=0)
    frobenius = jnp.sqrt(jnp.sum(squares, keepdims=True)[:1, :1])
    norm_scale = math.sqrt(order_full) / (2.0 * frobenius)
    row_ids = lax.broadcasted_iota(jnp.int32, (band_rows, band_cols), 0)
    col_ids = lax.broadcasted_iota(jnp.int32, (band_rows, band_cols), 1)
    for band in range(replicas):
        for shard in range(shards):
            tile = (stat[band, shard, 0].astype(jnp.float32) * norm_scale).astype(jnp.bfloat16)
            rows, columns = pl.ds(band * band_rows, band_rows), pl.ds(shard * band_cols, band_cols)
            scaled[rows, columns] = tile
            rest = -0.5 * tile.astype(jnp.float32)
            if (band * band_rows) // band_cols == shard:
                diagonal = row_ids + (band * band_rows - shard * band_cols) == col_ids
                rest = rest + jnp.where(diagonal, 1.5, 0.0)
            factor[rows, columns] = rest.astype(jnp.bfloat16)
    first = pl.multiple_of(place[0] * band_rows, band_rows)
    mine = factor[pl.ds(first, band_rows), :]
    product = jnp.dot(mine, scaled[...], preferred_element_type=jnp.float32).astype(jnp.bfloat16)
    product = jnp.dot(product, factor[...], preferred_element_type=jnp.float32)
    wide_rows = lax.broadcasted_iota(jnp.int32, (band_rows, order_full), 0) + first
    wide_cols = lax.broadcasted_iota(jnp.int32, (band_rows, order_full), 1)
    update = jnp.where(wide_rows == wide_cols, 1.5, 0.0) - 0.5 * product
    second = jnp.dot(update.astype(jnp.bfloat16), factor[...], preferred_element_type=jnp.float32)
    root = jnp.where(need[block] >= ITERS, second, mine.astype(jnp.float32)).astype(jnp.bfloat16)
    total = jnp.zeros((band_rows, band_cols), jnp.float32)
    for band in range(replicas):
        total = total + jnp.dot(
            root[:, band * band_rows : (band + 1) * band_rows],
            cols[band, 0, 0],
            preferred_element_type=jnp.float32,
        )
    out[0] = total.astype(jnp.bfloat16)


def newton_tile(place, need, stat, gathered):
    replicas, shards, home_count, band_rows, band_cols = stat.shape
    order_full = replicas * band_rows
    return pl.pallas_call(
        newton_kernel,
        out_shape=jax.ShapeDtypeStruct((home_count, band_rows, band_cols), jnp.bfloat16),
        grid_spec=pltpu.PrefetchScalarGridSpec(
            num_scalar_prefetch=2,
            grid=(home_count,),
            in_specs=[
                pl.BlockSpec(
                    (replicas, shards, 1, band_rows, band_cols),
                    lambda i, place, need: (0, 0, i, 0, 0),
                ),
                pl.BlockSpec(
                    (replicas, 1, 1, band_rows, band_cols),
                    lambda i, place, need: (0, place[1], i, 0, 0),
                ),
            ],
            out_specs=pl.BlockSpec((1, band_rows, band_cols), lambda i, place, need: (i, 0, 0)),
            scratch_shapes=[
                pltpu.VMEM((order_full, order_full), jnp.bfloat16),
                pltpu.VMEM((order_full, order_full), jnp.bfloat16),
            ],
        ),
        compiler_params=BIG,
    )(place, need, stat, gathered)


def exchange(array, axis):
    return lax.all_to_all(array, axis, split_axis=0, concat_axis=0, tiled=True)


def after(array, other):
    return lax.optimization_barrier((array, other))[0]


def body(partial_grads, owner_map, iterations, slot_history):
    owners = lax.axis_size(OWN)
    replicas = lax.axis_size(REP)
    shards = lax.axis_size(BLK)
    levels = lax.axis_size("zl")
    turns = lax.axis_size("y")
    my_rep, my_own, my_blk = lax.axis_index(REP), lax.axis_index(OWN), lax.axis_index(BLK)
    my_level, my_turn = lax.axis_index("zl"), lax.axis_index("y")
    _, home_count, order_full, band_cols = partial_grads.shape
    band_rows = order_full // replicas
    total_blocks = owner_map.shape[0]
    history = slot_history[0, 0]
    place = jnp.stack([my_rep, my_blk]).astype(jnp.int32)

    outgoing = (
        partial_grads[0]
        .reshape(home_count, replicas, band_rows, band_cols)
        .transpose(1, 0, 2, 3)
    )
    partials = exchange(outgoing, REP)
    grad_tile = jnp.sum(partials.astype(jnp.float32), axis=0).astype(jnp.bfloat16)

    position = jnp.arange(total_blocks, dtype=jnp.int32)
    same = owner_map[:, None] == owner_map[None, :]
    slot = jnp.sum(jnp.where(same & (position[None, :] < position[:, None]), 1, 0), axis=1)
    place_ids = jnp.arange(owners * shards, dtype=jnp.int32)
    lands = (owner_map * shards + slot)[None, :] == place_ids[:, None]
    holder = jnp.sum(jnp.where(lands, position[None, :] + 1, 0), axis=1).reshape(owners, shards) - 1
    my_holder = lax.dynamic_index_in_dim(holder, my_own, 0, keepdims=False)
    my_owners = lax.dynamic_slice_in_dim(owner_map, my_own * home_count, home_count)
    my_need = lax.dynamic_slice_in_dim(iterations, my_own * home_count, home_count)
    owner_ids = jnp.arange(owners, dtype=jnp.int32)
    slot_ids = jnp.arange(shards, dtype=jnp.int32)
    sits = (my_holder // home_count)[None, :] == owner_ids[:, None]
    slot_for_home = jnp.sum(jnp.where(sits & (my_holder >= 0)[None, :], slot_ids[None, :], 0), axis=1)

    history_tiles = exchange(cut_rows(place, history, shards, band_rows), BLK)

    grad_band = lax.all_gather(grad_tile, BLK, axis=0, tiled=False)
    grad_full = lax.all_gather(grad_band, REP, axis=0, tiled=False)

    history_sent = take(after(history_tiles, grad_band), slot_for_home)
    history_came = exchange(history_sent, OWN)

    gram, gram_half = gram_tile(place, grad_band, grad_full)
    tile = stat_tile(place, my_owners, gram, history_came)
    stat_band = lax.all_gather(tile, BLK, axis=0, tiled=False)
    stat_full = lax.all_gather(stat_band, REP, axis=0, tiled=False)

    column = lax.all_gather(gram_half, "y", axis=0, tiled=True)
    ring_size = shards * levels
    steps = (0, 1, -1, 2)

    def spot(height):
        height = height % ring_size
        return (height % levels) * shards + height // levels

    wanted = holder.reshape(levels, turns, shards)[:, my_turn]
    wanted_home = jnp.maximum(wanted, 0) // home_count
    in_column = (wanted_home % turns) * home_count + jnp.maximum(wanted, 0) % home_count
    arrivals = []
    for step in steps:
        level = lax.rem(my_level + step + levels, levels)
        sent = take(column, lax.dynamic_index_in_dim(in_column, level, 0, keepdims=False))
        if step:
            ring = [(spot(i), spot(i + step)) for i in range(ring_size)]
            sent = lax.ppermute(sent, RING, ring)
        arrivals.append(sent)
    my_from = jnp.maximum(my_holder, 0) // home_count // turns
    way = lax.rem(my_level - my_from + levels, levels)
    slot_step = jnp.where(way == 0, 0, jnp.where(way == 1, 1, jnp.where(way == 2, 3, 2)))
    slot_gram = take(jnp.concatenate(arrivals, axis=0), slot_step * shards + slot_ids)
    rows_gram = exchange(slot_gram, BLK)
    my_way = lax.dynamic_index_in_dim(way, my_blk, 0, keepdims=False)
    signed = jnp.where(my_way == levels - 1, -1, my_way)
    source = my_level - signed
    carry = jnp.where(source < 0, -1, jnp.where(source >= levels, 1, 0))
    occupied = jnp.where(lax.dynamic_index_in_dim(my_holder, my_blk, 0, keepdims=False) >= 0, 1, 0)
    turn = lax.rem(shards - carry, shards)
    new_rows = fresh_rows(jnp.stack([my_rep, turn, occupied]).astype(jnp.int32), history, rows_gram)

    directions = newton_tile(place, my_need, stat_full, grad_full)
    return (directions, new_rows[None, None])


def solution(mesh):
    fine = Mesh(mesh.devices.reshape(4, 2, 4, 8, 4), ("x", "core", "zl", "y", "zh"))
    return jax.shard_map(
        body,
        mesh=fine,
        in_specs=(P(REP, OWN, None, BLK), P(), P(), P(OWN, BLK, None, None)),
        out_specs=(P(OWN, REP, BLK), P(OWN, BLK, REP, None)),
        check_vma=False,
    )
```

```python
import math

import jax
import jax.numpy as jnp
from jax import lax
from jax.experimental import pallas as pl
from jax.experimental.pallas import tpu as pltpu
from jax.sharding import PartitionSpec as P

ITERS = 2


DECAY = 0.5
DAMPING = 0.05

BIG = pltpu.CompilerParams(vmem_limit_bytes=40 * 1024 * 1024)
SCALARS = pl.BlockSpec(memory_space=pltpu.SMEM)
WHOLE = pl.BlockSpec(memory_space=pltpu.VMEM)

REP_AT, BLK_AT, OWNER_AT, NEED_AT, HOLDER_AT = 0, 1, 2, 4, 6


def ds(start, size, unit):
    return pl.ds(pl.multiple_of(start, unit), size)


def pieces(tile, shards):
    depth = (4 * tile + tile // 2) // shards
    ends = sorted(set(range(0, shards * depth + 1, depth)) | set(range(0, 4 * tile + 1, tile)))
    return [
        (low // depth, low % depth, low // tile, low % tile, high - low)
        for low, high in zip(ends[:-1], ends[1:])
    ]


def call(kernel, ins, outs, in_specs=None, scratch=()):
    many = isinstance(outs, (list, tuple))
    return pl.pallas_call(
        kernel,
        out_shape=outs,
        in_specs=in_specs or [SCALARS] + [WHOLE] * (len(ins) - 1),
        out_specs=[WHOLE] * len(outs) if many else WHOLE,
        scratch_shapes=list(scratch),
        compiler_params=BIG,
    )(*ins)


def like(shape, dtype=jnp.bfloat16):
    return jax.ShapeDtypeStruct(shape, dtype)


def history_kernel(place, column, half, *refs):
    outs, held = refs[:-1], refs[-1]
    shards, depth, tile = held.shape
    for part, row, step, inner, size in pieces(tile, shards):
        if step < 4:
            start = lax.rem(place[0] + step, 8) * tile + inner
            held[part, row : row + size] = column[ds(start, size, 16), :]
        else:
            held[part, row : row + size] = half[inner : inner + size]
    for step in range(shards):
        outs[step][...] = held[lax.rem(place[1] + step, shards)]


def cut_history(place, history, shards, tile):
    depth = (4 * tile + tile // 2) // shards
    order_full = history.shape[0]
    return pl.pallas_call(
        history_kernel,
        out_shape=[like((depth, tile))] * shards,
        grid_spec=pltpu.PrefetchScalarGridSpec(
            num_scalar_prefetch=1,
            grid=(1,),
            in_specs=[
                pl.BlockSpec((order_full, tile), lambda i, place: (0, place[0])),
                pl.BlockSpec(
                    (tile // 2, tile),
                    lambda i, place: (
                        (lax.rem(place[0], 4) + 4) * 2 + place[0] // 4,
                        lax.rem(place[0], 4),
                    ),
                ),
            ],
            out_specs=[pl.BlockSpec((depth, tile), lambda i, place: (0, 0))] * shards,
            scratch_shapes=[pltpu.VMEM((shards, depth, tile), jnp.bfloat16)],
        ),
        compiler_params=BIG,
    )(place, history, history)


def spread_kernel(table, *refs):
    arrived, out = refs[:-1], refs[-1]
    shards = len(arrived)
    out[...] = jnp.zeros_like(out)
    for step in range(shards):
        holder = table[HOLDER_AT + lax.rem(table[BLK_AT] + shards - step, shards)]

        @pl.when(holder >= 0)
        def _(step=step, holder=holder):
            out[lax.div(holder, 2)] = arrived[step][...]


def gram_kernel(place, cols, *refs):
    outs, held = refs[:-1], refs[-1]
    shards, home_count, depth, tile = held.shape
    order_full = cols.shape[0] * tile
    rep = place[0]
    quarter = lax.rem(rep, 4)
    for block in range(home_count):
        mine = cols[rep, block]
        tiles = []
        for step in range(5):
            if step < 4:
                left, right = cols[lax.rem(rep + step, 8), block], mine
            else:
                start = lax.div(rep, 4) * (tile // 2)
                left = cols[quarter + 4, block, ds(start, tile // 2, 16), :]
                right = cols[quarter, block]
            product = lax.dot_general(
                left, right, (((1,), (1,)), ((), ())), preferred_element_type=jnp.float32
            )
            tiles.append((product * ((1.0 - DECAY) / order_full)).astype(jnp.bfloat16))
        for part, row, step, inner, size in pieces(tile, shards):
            held[part, block, row : row + size] = tiles[step][inner : inner + size]
    for step in range(shards):
        outs[step][...] = held[lax.rem(place[1] + step, shards)]


def add_kernel(table, *refs):
    arrived, total_out, sent = refs[:-2], refs[-2], refs[-1]
    total = sum(ref[...].astype(jnp.float32) for ref in arrived)
    total_out[...] = total
    sent[...] = jnp.zeros_like(sent)
    for block in range(total.shape[0]):
        sent[table[OWNER_AT + block]] = total[block].astype(jnp.bfloat16)


def stat_kernel(table, gram, came, out):
    home_count, depth, tile = out.shape
    row_ids = lax.broadcasted_iota(jnp.int32, (depth, tile), 0)
    col_ids = lax.broadcasted_iota(jnp.int32, (depth, tile), 1)
    damping = jnp.where((row_ids + table[BLK_AT] * depth) == col_ids, DAMPING, 0.0)
    for block in range(home_count):
        history = came[table[OWNER_AT + block]].astype(jnp.float32)
        out[block] = (DECAY * history + gram[block] + damping).astype(jnp.bfloat16)


def order_kernel(table, *refs):
    arrived, out = refs[:-1], refs[-1]
    shards = len(arrived)
    for step in range(shards):
        out[lax.rem(table[BLK_AT] + shards - step, shards)] = arrived[step][...]


def choose_kernel(table, came, *outs):
    shards = len(outs)
    for step in range(shards):
        holder = table[HOLDER_AT + lax.rem(table[BLK_AT] + step, shards)]
        outs[step][...] = came[lax.div(jnp.maximum(holder, 0), 2)]


def turn_kernel(table, *refs):
    arrived, band, sent = refs[:-2], refs[-2], refs[-1]
    shards = len(arrived)
    depth, tile = arrived[0].shape
    for step in range(shards):
        part = lax.rem(table[BLK_AT] + shards - step, shards)
        band[ds(part * depth, depth, 16), :] = arrived[step][...]
    sent[...] = jnp.zeros_like(sent)
    for step in range(1, 4):
        sent[lax.rem(table[REP_AT] + step, 8)] = band[step * tile : (step + 1) * tile]
    sent[lax.rem(table[REP_AT] + 4, 8), : tile // 2] = band[4 * tile :]


def finish_kernel(place, rows, band, came, out):
    tile = rows.shape[0]
    rep = place[0]
    first = rep < 4

    def put(column, gram, damping=None):
        columns = ds(column * tile, tile, tile)
        history = rows[:, columns].astype(jnp.float32)
        fresh = DECAY * history + gram
        if damping is not None:
            fresh = fresh + damping
        out[:, columns] = jnp.where(place[1] > 0, fresh, history).astype(jnp.bfloat16)

    row_ids = lax.broadcasted_iota(jnp.int32, (tile, tile), 0)
    col_ids = lax.broadcasted_iota(jnp.int32, (tile, tile), 1)
    put(rep, band[:tile].astype(jnp.float32), jnp.where(row_ids == col_ids, DAMPING, 0.0))
    for step in range(1, 4):
        mine = band[step * tile : (step + 1) * tile].astype(jnp.float32)
        put(lax.rem(rep + step, 8), mine.T)
        other = lax.rem(rep + 8 - step, 8)
        put(other, came[other].astype(jnp.float32))
    other = lax.rem(rep + 4, 8)
    mine = band[4 * tile :].astype(jnp.float32)
    theirs = came[other, : tile // 2].astype(jnp.float32)
    upper, lower = jnp.where(first, mine, theirs), jnp.where(first, theirs, mine)
    whole = jnp.concatenate([upper, lower], axis=0)
    put(other, jnp.where(first, whole.T, whole))


def finish(place, history, band, came):
    tile, order_full = band.shape[1], history.shape[1]
    return pl.pallas_call(
        finish_kernel,
        out_shape=like((tile, order_full)),
        grid_spec=pltpu.PrefetchScalarGridSpec(
            num_scalar_prefetch=1,
            grid=(1,),
            in_specs=[
                pl.BlockSpec((tile, order_full), lambda i, place: (place[0], 0)),
                pl.BlockSpec(band.shape, lambda i, place: (0, 0)),
                pl.BlockSpec(came.shape, lambda i, place: (0, 0, 0)),
            ],
            out_specs=pl.BlockSpec((tile, order_full), lambda i, place: (0, 0)),
        ),
        compiler_params=BIG,
    )(place, history, band, came)


def newton_kernel(table, stat, cols, out, full):
    bands, shards, _, depth, tile = stat.shape
    order_full = bands * tile
    block = pl.program_id(0)
    squares = jnp.zeros((8, tile), jnp.float32)
    for band in range(bands):
        for shard in range(shards):
            part = stat[band, shard, 0].astype(jnp.float32)
            squares = squares + 2.0 * jnp.sum((part * part).reshape(-1, 8, tile), axis=0)
        part = stat[band, 0, 0, :tile].astype(jnp.float32)
        squares = squares - jnp.sum((part * part).reshape(-1, 8, tile), axis=0)
    frobenius = jnp.sqrt(jnp.sum(squares, keepdims=True)[:1, :1])
    norm_scale = math.sqrt(order_full) / (2.0 * frobenius)

    def at(index):
        return slice(index * tile, (index + 1) * tile)

    for band in range(bands):
        for part, row, step, inner, size in pieces(tile, shards):
            if step < 4:
                start, columns = (band + step) % bands * tile + inner, at(band)
            else:
                start = (band % 4 + 4) * tile + band // 4 * (tile // 2) + inner
                columns = at(band % 4)
            piece = stat[band, part, 0, row : row + size].astype(jnp.float32) * norm_scale
            full[start : start + size, columns] = piece.astype(jnp.bfloat16)
    for band in range(bands):
        for step in range(1, 5 if band < 4 else 4):
            other = (band + step) % bands
            full[at(band), at(other)] = full[at(other), at(band)].T

    row_ids = lax.broadcasted_iota(jnp.int32, (tile, tile), 0)
    col_ids = lax.broadcasted_iota(jnp.int32, (tile, tile), 1)
    diagonals = []
    for band in range(bands):
        corner = full[at(band), at(band)].astype(jnp.float32)
        values = jnp.sum(jnp.where(row_ids == col_ids, corner, 0.0), axis=0, keepdims=True)
        rounded = (1.5 - 0.5 * values).astype(jnp.bfloat16).astype(jnp.float32)
        diagonals.append(rounded + 0.5 * values)
    diagonal = jnp.concatenate(diagonals, axis=1)

    def times_scaled(left):
        return jnp.dot(left, full[...], preferred_element_type=jnp.float32)

    def times_factor(left):
        return left.astype(jnp.float32) * diagonal - 0.5 * times_scaled(left)

    first = table[REP_AT] * tile
    wide_rows = lax.broadcasted_iota(jnp.int32, (tile, order_full), 0) + first
    wide_cols = lax.broadcasted_iota(jnp.int32, (tile, order_full), 1)
    identity = jnp.where(wide_rows == wide_cols, 1.5, 0.0)
    mine = full[ds(first, tile, tile), :].astype(jnp.float32)
    mine = (identity - 0.5 * mine).astype(jnp.bfloat16)
    product = times_factor(times_scaled(mine).astype(jnp.bfloat16))
    update = (identity - 0.5 * product).astype(jnp.bfloat16)
    second = times_factor(update).astype(jnp.bfloat16)
    root = jnp.where(table[NEED_AT + block] >= ITERS, second, mine)
    total = jnp.zeros(out.shape[1:], jnp.float32)
    for band in range(bands):
        total = total + jnp.dot(root[:, at(band)], cols[band, 0], preferred_element_type=jnp.float32)
    out[0] = total.astype(jnp.bfloat16)


def newton(table, stat, cols):
    bands, shards, home_count, depth, tile = stat.shape
    width = cols.shape[3]
    return pl.pallas_call(
        newton_kernel,
        out_shape=like((home_count, tile, width)),
        grid_spec=pltpu.PrefetchScalarGridSpec(
            num_scalar_prefetch=1,
            grid=(home_count,),
            in_specs=[
                pl.BlockSpec((bands, shards, 1, depth, tile), lambda i, table: (0, 0, i, 0, 0)),
                pl.BlockSpec((bands, 1, tile, width), lambda i, table: (0, i, 0, 0)),
            ],
            out_specs=pl.BlockSpec((1, tile, width), lambda i, table: (i, 0, 0)),
            scratch_shapes=[pltpu.VMEM((bands * tile, bands * tile), jnp.bfloat16)],
        ),
        compiler_params=BIG,
    )(table, stat, cols)


def exchange(array, axis):
    return lax.all_to_all(array, axis, split_axis=0, concat_axis=0, tiled=True)


def swap(parts, count):
    return [parts[0]] + [
        lax.ppermute(parts[step], "blk", [(i, (i + step) % count) for i in range(count)])
        for step in range(1, count)
    ]


def after(array, other):
    return lax.optimization_barrier((array, other))[0]


def body(partial_grads, owner_map, iterations, slot_history):
    owners = lax.axis_size("own")
    replicas = lax.axis_size("rep")
    shards = lax.axis_size("blk")
    my_rep, my_own, my_blk = lax.axis_index("rep"), lax.axis_index("own"), lax.axis_index("blk")
    _, home_count, order_full, band_cols = partial_grads.shape
    tile = order_full // replicas
    depth = (4 * tile + tile // 2) // shards
    total_blocks = owner_map.shape[0]
    history = slot_history[0, 0]
    place = jnp.stack([my_rep, my_blk]).astype(jnp.int32)

    position = jnp.arange(total_blocks, dtype=jnp.int32)
    same = owner_map[:, None] == owner_map[None, :]
    slot = jnp.sum(jnp.where(same & (position[None, :] < position[:, None]), 1, 0), axis=1)
    slot_ids = jnp.arange(shards, dtype=jnp.int32)
    held = (owner_map[None, :] == my_own) & (slot[None, :] == slot_ids[:, None])
    holder = jnp.sum(jnp.where(held, position[None, :] + 1, 0), axis=1) - 1
    my_owners = lax.dynamic_slice_in_dim(owner_map, my_own * home_count, home_count)
    my_need = lax.dynamic_slice_in_dim(iterations, my_own * home_count, home_count)
    table = jnp.concatenate([place, my_owners, my_need, holder]).astype(jnp.int32)

    outgoing = (
        partial_grads[0].reshape(home_count, replicas, tile, band_cols).transpose(1, 0, 2, 3)
    )
    history_parts = cut_history(place, history, shards, tile)
    history_arrived = swap(history_parts, shards)
    partials = exchange(outgoing, "rep")
    grad_tile = jnp.sum(partials.astype(jnp.float32), axis=0).astype(jnp.bfloat16)
    grad_cols = lax.all_gather(grad_tile, "rep", axis=0, tiled=False)

    history_sent = call(spread_kernel, [table, *history_arrived], like((owners, depth, tile)))
    history_came = exchange(after(history_sent, grad_tile), "own")

    gram_parts = pl.pallas_call(
        gram_kernel,
        out_shape=[like((home_count, depth, tile))] * shards,
        in_specs=[SCALARS, WHOLE],
        out_specs=[WHOLE] * shards,
        scratch_shapes=[pltpu.VMEM((shards, home_count, depth, tile), jnp.bfloat16)],
        compiler_params=BIG,
    )(place, grad_cols)
    gram_arrived = swap(gram_parts, shards)
    gram, gram_sent = call(
        add_kernel,
        [table, *gram_arrived],
        [like((home_count, depth, tile), jnp.float32), like((owners, depth, tile))],
    )
    stat = call(stat_kernel, [table, gram, history_came], like((home_count, depth, tile)))
    stat_band = call(
        order_kernel, [table, *swap([stat] * shards, shards)], like((shards, home_count, depth, tile))
    )
    stat_full = lax.all_gather(stat_band, "rep", axis=0, tiled=False)

    gram_came = exchange(after(gram_sent, stat), "own")
    slot_parts = call(choose_kernel, [table, gram_came], [like((depth, tile))] * shards)
    band, turned = call(
        turn_kernel,
        [table, *swap(slot_parts, shards)],
        [like((shards * depth, tile)), like((replicas, tile, tile))],
    )
    turned = exchange(turned, "rep")
    occupied = jnp.where(lax.dynamic_index_in_dim(holder, my_blk, 0, keepdims=False) >= 0, 1, 0)
    new_rows = finish(jnp.stack([my_rep, occupied]).astype(jnp.int32), history, band, turned)

    directions = newton(table, stat_full, grad_cols)
    return (directions, new_rows[None, None])


def solution(mesh):
    return jax.shard_map(
        body,
        mesh=mesh,
        in_specs=(P("rep", "own", None, "blk"), P(), P(), P("own", "blk", None, None)),
        out_specs=(P("own", "rep", "blk"), P("own", "blk", "rep", None)),
        check_vma=False,
    )
```

```python
import math

import jax
import jax.numpy as jnp
from jax import lax
from jax.experimental import pallas as pl
from jax.experimental.pallas import tpu as pltpu
from jax.sharding import PartitionSpec as P

ITERS = 2


DECAY = 0.5
DAMPING = 0.05

BIG = pltpu.CompilerParams(vmem_limit_bytes=40 * 1024 * 1024)
SCALARS = pl.BlockSpec(memory_space=pltpu.SMEM)
WHOLE = pl.BlockSpec(memory_space=pltpu.VMEM)

REP_AT, BLK_AT, OWNER_AT, NEED_AT, HOLDER_AT = 0, 1, 2, 4, 6


def ds(start, size, unit):
    return pl.ds(pl.multiple_of(start, unit), size)


def pieces(tile, shards):
    depth = (4 * tile + tile // 2) // shards
    ends = sorted(set(range(0, shards * depth + 1, depth)) | set(range(0, 4 * tile + 1, tile)))
    return [
        (low // depth, low % depth, low // tile, low % tile, high - low)
        for low, high in zip(ends[:-1], ends[1:])
    ]


def call(kernel, ins, outs, in_specs=None, scratch=()):
    many = isinstance(outs, (list, tuple))
    return pl.pallas_call(
        kernel,
        out_shape=outs,
        in_specs=in_specs or [SCALARS] + [WHOLE] * (len(ins) - 1),
        out_specs=[WHOLE] * len(outs) if many else WHOLE,
        scratch_shapes=list(scratch),
        compiler_params=BIG,
    )(*ins)


def like(shape, dtype=jnp.bfloat16):
    return jax.ShapeDtypeStruct(shape, dtype)


def split_kernel(grads, out, sems):
    copies = []
    for band in range(out.shape[0]):
        for block in range(out.shape[1]):
            rows = pl.ds(band * out.shape[2], out.shape[2])
            copies.append(
                pltpu.make_async_copy(grads.at[block, rows], out.at[band, block], sems.at[band, block])
            )
    for copy in copies:
        copy.start()
    for copy in copies:
        copy.wait()


def split_bands(grads, replicas):
    home_count, order_full, width = grads.shape
    return pl.pallas_call(
        split_kernel,
        out_shape=like((replicas, home_count, order_full // replicas, width)),
        in_specs=[pl.BlockSpec(memory_space=pl.ANY)],
        out_specs=pl.BlockSpec(memory_space=pl.ANY),
        scratch_shapes=[pltpu.SemaphoreType.DMA((replicas, home_count))],
    )(grads)


def history_kernel(place, column, half, out):
    tile = column.shape[1]
    for step in range(4):
        out[step * tile : (step + 1) * tile] = column[ds(lax.rem(place[0] + step, 8) * tile, tile, tile), :]
    out[4 * tile : 4 * tile + tile // 2] = half[...]


def cut_history(place, history, tile):
    order_full = history.shape[0]
    shape = (order_full, tile)
    return pl.pallas_call(
        history_kernel,
        out_shape=like(shape),
        grid_spec=pltpu.PrefetchScalarGridSpec(
            num_scalar_prefetch=1,
            grid=(1,),
            in_specs=[
                pl.BlockSpec((order_full, tile), lambda i, place: (0, place[0])),
                pl.BlockSpec(
                    (tile // 2, tile),
                    lambda i, place: (
                        (lax.rem(place[0], 4) + 4) * 2 + place[0] // 4,
                        lax.rem(place[0], 4),
                    ),
                ),
            ],
            out_specs=pl.BlockSpec(shape, lambda i, place: (0, 0)),
        ),
        compiler_params=BIG,
    )(place, history, history)


def spread_kernel(table, bands, out):
    depth = out.shape[1]
    start = table[BLK_AT] * depth
    out[...] = jnp.zeros_like(out)
    for shard in range(bands.shape[0]):
        holder = table[HOLDER_AT + shard]

        @pl.when(holder >= 0)
        def _(shard=shard, holder=holder):
            out[lax.div(holder, 2)] = bands[shard, ds(start, depth, 16), :]


def gram_kernel(place, cols, *refs):
    outs, held = refs[:-1], refs[-1]
    shards, home_count, depth, tile = held.shape
    order_full = cols.shape[0] * tile
    rep = place[0]
    quarter = lax.rem(rep, 4)
    for block in range(home_count):
        mine = cols[rep, block]
        tiles = []
        for step in range(5):
            if step < 4:
                left, right = cols[lax.rem(rep + step, 8), block], mine
            else:
                start = lax.div(rep, 4) * (tile // 2)
                left = cols[quarter + 4, block, ds(start, tile // 2, 16), :]
                right = cols[quarter, block]
            product = lax.dot_general(
                left, right, (((1,), (1,)), ((), ())), preferred_element_type=jnp.float32
            )
            tiles.append((product * ((1.0 - DECAY) / order_full)).astype(jnp.bfloat16))
        for part, row, step, inner, size in pieces(tile, shards):
            held[part, block, row : row + size] = tiles[step][inner : inner + size]
    for step in range(shards):
        outs[step][...] = held[lax.rem(place[1] + step, shards)]


def add_kernel(table, *refs):
    arrived, total_out, sent = refs[:-2], refs[-2], refs[-1]
    total = sum(ref[...].astype(jnp.float32) for ref in arrived)
    total_out[...] = total
    sent[...] = jnp.zeros_like(sent)
    for block in range(total.shape[0]):
        sent[table[OWNER_AT + block]] = total[block].astype(jnp.bfloat16)


def stat_kernel(table, gram, came, out):
    home_count, depth, tile = out.shape
    row_ids = lax.broadcasted_iota(jnp.int32, (depth, tile), 0)
    col_ids = lax.broadcasted_iota(jnp.int32, (depth, tile), 1)
    damping = jnp.where((row_ids + table[BLK_AT] * depth) == col_ids, DAMPING, 0.0)
    for block in range(home_count):
        history = came[table[OWNER_AT + block]].astype(jnp.float32)
        out[block] = (DECAY * history + gram[block] + damping).astype(jnp.bfloat16)


def choose_kernel(table, came, out):
    for shard in range(out.shape[0]):
        out[shard] = came[lax.div(jnp.maximum(table[HOLDER_AT + shard], 0), 2)]


def turn_kernel(table, parts, band, sent):
    shards, depth, tile = parts.shape
    for part in range(shards):
        band[part * depth : (part + 1) * depth] = parts[part]
    sent[...] = jnp.zeros_like(sent)
    for step in range(1, 4):
        sent[lax.rem(table[REP_AT] + step, 8)] = band[step * tile : (step + 1) * tile]
    sent[lax.rem(table[REP_AT] + 4, 8), : tile // 2] = band[4 * tile :]


def finish_kernel(place, rows, band, came, out):
    tile = rows.shape[0]
    rep = place[0]
    first = rep < 4

    def put(column, gram, damping=None):
        columns = ds(column * tile, tile, tile)
        history = rows[:, columns].astype(jnp.float32)
        fresh = DECAY * history + gram
        if damping is not None:
            fresh = fresh + damping
        out[:, columns] = jnp.where(place[1] > 0, fresh, history).astype(jnp.bfloat16)

    row_ids = lax.broadcasted_iota(jnp.int32, (tile, tile), 0)
    col_ids = lax.broadcasted_iota(jnp.int32, (tile, tile), 1)
    put(rep, band[:tile].astype(jnp.float32), jnp.where(row_ids == col_ids, DAMPING, 0.0))
    for step in range(1, 4):
        mine = band[step * tile : (step + 1) * tile].astype(jnp.float32)
        put(lax.rem(rep + step, 8), mine.T)
        other = lax.rem(rep + 8 - step, 8)
        put(other, came[other].astype(jnp.float32))
    other = lax.rem(rep + 4, 8)
    mine = band[4 * tile :].astype(jnp.float32)
    theirs = came[other, : tile // 2].astype(jnp.float32)
    upper, lower = jnp.where(first, mine, theirs), jnp.where(first, theirs, mine)
    whole = jnp.concatenate([upper, lower], axis=0)
    put(other, jnp.where(first, whole.T, whole))


def finish(place, history, band, came):
    tile, order_full = band.shape[1], history.shape[1]
    return pl.pallas_call(
        finish_kernel,
        out_shape=like((tile, order_full)),
        grid_spec=pltpu.PrefetchScalarGridSpec(
            num_scalar_prefetch=1,
            grid=(1,),
            in_specs=[
                pl.BlockSpec((tile, order_full), lambda i, place: (place[0], 0)),
                pl.BlockSpec(band.shape, lambda i, place: (0, 0)),
                pl.BlockSpec(came.shape, lambda i, place: (0, 0, 0)),
            ],
            out_specs=pl.BlockSpec((tile, order_full), lambda i, place: (0, 0)),
        ),
        compiler_params=BIG,
    )(place, history, band, came)


def newton_kernel(table, stat, cols, out, full):
    bands, shards, _, depth, tile = stat.shape
    order_full = bands * tile
    block = pl.program_id(0)
    squares = jnp.zeros((8, tile), jnp.float32)
    for band in range(bands):
        for shard in range(shards):
            part = stat[band, shard, 0].astype(jnp.float32)
            squares = squares + 2.0 * jnp.sum((part * part).reshape(-1, 8, tile), axis=0)
        part = stat[band, 0, 0, :tile].astype(jnp.float32)
        squares = squares - jnp.sum((part * part).reshape(-1, 8, tile), axis=0)
    frobenius = jnp.sqrt(jnp.sum(squares, keepdims=True)[:1, :1])
    norm_scale = math.sqrt(order_full) / (2.0 * frobenius)

    def at(index):
        return slice(index * tile, (index + 1) * tile)

    for band in range(bands):
        for part, row, step, inner, size in pieces(tile, shards):
            if step < 4:
                start, columns = (band + step) % bands * tile + inner, at(band)
            else:
                start = (band % 4 + 4) * tile + band // 4 * (tile // 2) + inner
                columns = at(band % 4)
            piece = stat[band, part, 0, row : row + size].astype(jnp.float32) * norm_scale
            full[start : start + size, columns] = piece.astype(jnp.bfloat16)
    for band in range(bands):
        for step in range(1, 5 if band < 4 else 4):
            other = (band + step) % bands
            full[at(band), at(other)] = full[at(other), at(band)].T

    row_ids = lax.broadcasted_iota(jnp.int32, (tile, tile), 0)
    col_ids = lax.broadcasted_iota(jnp.int32, (tile, tile), 1)
    diagonals = []
    for band in range(bands):
        corner = full[at(band), at(band)].astype(jnp.float32)
        values = jnp.sum(jnp.where(row_ids == col_ids, corner, 0.0), axis=0, keepdims=True)
        rounded = (1.5 - 0.5 * values).astype(jnp.bfloat16).astype(jnp.float32)
        diagonals.append(rounded + 0.5 * values)
    diagonal = jnp.concatenate(diagonals, axis=1)

    def times_scaled(left):
        return jnp.dot(left, full[...], preferred_element_type=jnp.float32)

    def times_factor(left):
        return left.astype(jnp.float32) * diagonal - 0.5 * times_scaled(left)

    first = table[REP_AT] * tile
    wide_rows = lax.broadcasted_iota(jnp.int32, (tile, order_full), 0) + first
    wide_cols = lax.broadcasted_iota(jnp.int32, (tile, order_full), 1)
    identity = jnp.where(wide_rows == wide_cols, 1.5, 0.0)
    mine = full[ds(first, tile, tile), :].astype(jnp.float32)
    mine = (identity - 0.5 * mine).astype(jnp.bfloat16)
    product = times_factor(times_scaled(mine).astype(jnp.bfloat16))
    update = (identity - 0.5 * product).astype(jnp.bfloat16)
    second = times_factor(update).astype(jnp.bfloat16)
    root = jnp.where(table[NEED_AT + block] >= ITERS, second, mine)
    total = jnp.zeros(out.shape[1:], jnp.float32)
    for band in range(bands):
        total = total + jnp.dot(root[:, at(band)], cols[band, 0], preferred_element_type=jnp.float32)
    out[0] = total.astype(jnp.bfloat16)


def newton(table, stat, cols):
    bands, shards, home_count, depth, tile = stat.shape
    width = cols.shape[3]
    return pl.pallas_call(
        newton_kernel,
        out_shape=like((home_count, tile, width)),
        grid_spec=pltpu.PrefetchScalarGridSpec(
            num_scalar_prefetch=1,
            grid=(home_count,),
            in_specs=[
                pl.BlockSpec((bands, shards, 1, depth, tile), lambda i, table: (0, 0, i, 0, 0)),
                pl.BlockSpec((bands, 1, tile, width), lambda i, table: (0, i, 0, 0)),
            ],
            out_specs=pl.BlockSpec((1, tile, width), lambda i, table: (i, 0, 0)),
            scratch_shapes=[pltpu.VMEM((bands * tile, bands * tile), jnp.bfloat16)],
        ),
        compiler_params=BIG,
    )(table, stat, cols)


def exchange(array, axis):
    return lax.all_to_all(array, axis, split_axis=0, concat_axis=0, tiled=True)


def swap(parts, count):
    return [parts[0]] + [
        lax.ppermute(parts[step], "blk", [(i, (i + step) % count) for i in range(count)])
        for step in range(1, count)
    ]


def after(array, other):
    return lax.optimization_barrier((array, other))[0]


def body(partial_grads, owner_map, iterations, slot_history):
    owners = lax.axis_size("own")
    replicas = lax.axis_size("rep")
    shards = lax.axis_size("blk")
    my_rep, my_own, my_blk = lax.axis_index("rep"), lax.axis_index("own"), lax.axis_index("blk")
    _, home_count, order_full, band_cols = partial_grads.shape
    tile = order_full // replicas
    depth = (4 * tile + tile // 2) // shards
    total_blocks = owner_map.shape[0]
    history = slot_history[0, 0]
    place = jnp.stack([my_rep, my_blk]).astype(jnp.int32)

    position = jnp.arange(total_blocks, dtype=jnp.int32)
    same = owner_map[:, None] == owner_map[None, :]
    slot = jnp.sum(jnp.where(same & (position[None, :] < position[:, None]), 1, 0), axis=1)
    slot_ids = jnp.arange(shards, dtype=jnp.int32)
    held = (owner_map[None, :] == my_own) & (slot[None, :] == slot_ids[:, None])
    holder = jnp.sum(jnp.where(held, position[None, :] + 1, 0), axis=1) - 1
    my_owners = lax.dynamic_slice_in_dim(owner_map, my_own * home_count, home_count)
    my_need = lax.dynamic_slice_in_dim(iterations, my_own * home_count, home_count)
    table = jnp.concatenate([place, my_owners, my_need, holder]).astype(jnp.int32)

    outgoing = split_bands(partial_grads[0], replicas)
    history_bands = lax.all_gather(cut_history(place, history, tile), "blk", axis=0, tiled=False)
    partials = exchange(outgoing, "rep")
    grad_tile = jnp.sum(partials.astype(jnp.float32), axis=0).astype(jnp.bfloat16)
    grad_cols = exchange(jnp.broadcast_to(grad_tile[None], (replicas,) + grad_tile.shape), "rep")

    history_sent = call(spread_kernel, [table, history_bands], like((owners, depth, tile)))
    history_came = exchange(after(history_sent, grad_cols), "own")

    gram_parts = pl.pallas_call(
        gram_kernel,
        out_shape=[like((home_count, depth, tile))] * shards,
        in_specs=[SCALARS, WHOLE],
        out_specs=[WHOLE] * shards,
        scratch_shapes=[pltpu.VMEM((shards, home_count, depth, tile), jnp.bfloat16)],
        compiler_params=BIG,
    )(place, grad_cols)
    gram_arrived = swap(gram_parts, shards)
    gram, gram_sent = call(
        add_kernel,
        [table, *gram_arrived],
        [like((home_count, depth, tile), jnp.float32), like((owners, depth, tile))],
    )
    stat = call(stat_kernel, [table, gram, history_came], like((home_count, depth, tile)))
    gram_came = exchange(after(gram_sent, history_came), "own")
    stat_band = lax.all_gather(stat, "blk", axis=0, tiled=False)
    stat_full = lax.all_gather(stat_band, "rep", axis=0, tiled=False)

    slot_parts = call(choose_kernel, [table, gram_came], like((shards, depth, tile)))
    band, turned = call(
        turn_kernel,
        [table, exchange(slot_parts, "blk")],
        [like((shards * depth, tile)), like((replicas, tile, tile))],
    )
    turned = exchange(turned, "rep")
    occupied = jnp.where(lax.dynamic_index_in_dim(holder, my_blk, 0, keepdims=False) >= 0, 1, 0)
    new_rows = finish(jnp.stack([my_rep, occupied]).astype(jnp.int32), history, band, turned)

    directions = newton(table, stat_full, grad_cols)
    return (directions, new_rows[None, None])


def solution(mesh):
    return jax.shard_map(
        body,
        mesh=mesh,
        in_specs=(P("rep", "own", None, "blk"), P(), P(), P("own", "blk", None, None)),
        out_specs=(P("own", "rep", "blk"), P("own", "blk", "rep", None)),
        check_vma=False,
    )
```

```python
import math

import jax
import jax.numpy as jnp
from jax import lax
from jax.experimental import pallas as pl
from jax.experimental.pallas import tpu as pltpu
from jax.sharding import PartitionSpec as P

ITERS = 2


DECAY = 0.5
DAMPING = 0.05

BIG = pltpu.CompilerParams(vmem_limit_bytes=40 * 1024 * 1024)
SCALARS = pl.BlockSpec(memory_space=pltpu.SMEM)
WHOLE = pl.BlockSpec(memory_space=pltpu.VMEM)

REP_AT, BLK_AT, OWNER_AT, NEED_AT, HOLDER_AT = 0, 1, 2, 4, 6


def ds(start, size, unit):
    return pl.ds(pl.multiple_of(start, unit), size)


def pieces(tile, shards):
    depth = (4 * tile + tile // 2) // shards
    ends = sorted(set(range(0, shards * depth + 1, depth)) | set(range(0, 4 * tile + 1, tile)))
    return [
        (low // depth, low % depth, low // tile, low % tile, high - low)
        for low, high in zip(ends[:-1], ends[1:])
    ]


def call(kernel, ins, outs, in_specs=None, scratch=()):
    many = isinstance(outs, (list, tuple))
    return pl.pallas_call(
        kernel,
        out_shape=outs,
        in_specs=in_specs or [SCALARS] + [WHOLE] * (len(ins) - 1),
        out_specs=[WHOLE] * len(outs) if many else WHOLE,
        scratch_shapes=list(scratch),
        compiler_params=BIG,
    )(*ins)


def like(shape, dtype=jnp.bfloat16):
    return jax.ShapeDtypeStruct(shape, dtype)


def history_kernel(place, column, half, *refs):
    outs, held = refs[:-1], refs[-1]
    shards, depth, tile = held.shape
    for part, row, step, inner, size in pieces(tile, shards):
        if step < 4:
            start = lax.rem(place[0] + step, 8) * tile + inner
            held[part, row : row + size] = column[ds(start, size, 16), :]
        else:
            held[part, row : row + size] = half[inner : inner + size]
    for step in range(shards):
        outs[step][...] = held[lax.rem(place[1] + step, shards)]


def cut_history(place, history, shards, tile):
    depth = (4 * tile + tile // 2) // shards
    order_full = history.shape[0]
    return pl.pallas_call(
        history_kernel,
        out_shape=[like((depth, tile))] * shards,
        grid_spec=pltpu.PrefetchScalarGridSpec(
            num_scalar_prefetch=1,
            grid=(1,),
            in_specs=[
                pl.BlockSpec((order_full, tile), lambda i, place: (0, place[0])),
                pl.BlockSpec(
                    (tile // 2, tile),
                    lambda i, place: (
                        (lax.rem(place[0], 4) + 4) * 2 + place[0] // 4,
                        lax.rem(place[0], 4),
                    ),
                ),
            ],
            out_specs=[pl.BlockSpec((depth, tile), lambda i, place: (0, 0))] * shards,
            scratch_shapes=[pltpu.VMEM((shards, depth, tile), jnp.bfloat16)],
        ),
        compiler_params=BIG,
    )(place, history, history)


def spread_kernel(table, *refs):
    arrived, out = refs[:-1], refs[-1]
    shards = len(arrived)
    out[...] = jnp.zeros_like(out)
    for step in range(shards):
        holder = table[HOLDER_AT + lax.rem(table[BLK_AT] + shards - step, shards)]

        @pl.when(holder >= 0)
        def _(step=step, holder=holder):
            out[lax.div(holder, 2)] = arrived[step][...]


def gram_kernel(place, *refs):
    out = refs[-1]
    shards, home_count, depth, tile = out.shape
    order_full = refs[0].shape[0] * tile
    rep = place[0]
    quarter = lax.rem(rep, 4)
    for block in range(home_count):
        cols = refs[block]
        mine = cols[rep]
        tiles = []
        for step in range(5):
            if step < 4:
                left, right = cols[lax.rem(rep + step, 8)], mine
            else:
                start = lax.div(rep, 4) * (tile // 2)
                left = cols[quarter + 4, ds(start, tile // 2, 16), :]
                right = cols[quarter]
            product = lax.dot_general(
                left, right, (((1,), (1,)), ((), ())), preferred_element_type=jnp.float32
            )
            tiles.append((product * ((1.0 - DECAY) / order_full)).astype(jnp.bfloat16))
        for part, row, step, inner, size in pieces(tile, shards):
            out[part, block, row : row + size] = tiles[step][inner : inner + size]


def add_kernel(table, arrived, total_out, sent):
    total = jnp.sum(arrived[...].astype(jnp.float32), axis=0)
    total_out[...] = total
    sent[...] = jnp.zeros_like(sent)
    for block in range(total.shape[0]):
        sent[table[OWNER_AT + block]] = total[block].astype(jnp.bfloat16)


def stat_kernel(table, gram, came, out):
    home_count, depth, tile = out.shape
    row_ids = lax.broadcasted_iota(jnp.int32, (depth, tile), 0)
    col_ids = lax.broadcasted_iota(jnp.int32, (depth, tile), 1)
    damping = jnp.where((row_ids + table[BLK_AT] * depth) == col_ids, DAMPING, 0.0)
    for block in range(home_count):
        history = came[table[OWNER_AT + block]].astype(jnp.float32)
        out[block] = (DECAY * history + gram[block] + damping).astype(jnp.bfloat16)


def choose_kernel(table, came, out):
    for shard in range(out.shape[0]):
        out[shard] = came[lax.div(jnp.maximum(table[HOLDER_AT + shard], 0), 2)]


def turn_kernel(table, parts, band, sent):
    shards, depth, tile = parts.shape
    for part in range(shards):
        band[part * depth : (part + 1) * depth] = parts[part]
    sent[...] = jnp.zeros_like(sent)
    for step in range(1, 4):
        sent[lax.rem(table[REP_AT] + step, 8)] = band[step * tile : (step + 1) * tile]
    sent[lax.rem(table[REP_AT] + 4, 8), : tile // 2] = band[4 * tile :]


def finish_kernel(place, rows, band, came, out):
    tile = rows.shape[0]
    rep = place[0]
    first = rep < 4

    def put(column, gram, damping=None):
        columns = ds(column * tile, tile, tile)
        history = rows[:, columns].astype(jnp.float32)
        fresh = DECAY * history + gram
        if damping is not None:
            fresh = fresh + damping
        out[:, columns] = jnp.where(place[1] > 0, fresh, history).astype(jnp.bfloat16)

    row_ids = lax.broadcasted_iota(jnp.int32, (tile, tile), 0)
    col_ids = lax.broadcasted_iota(jnp.int32, (tile, tile), 1)
    put(rep, band[:tile].astype(jnp.float32), jnp.where(row_ids == col_ids, DAMPING, 0.0))
    for step in range(1, 4):
        mine = band[step * tile : (step + 1) * tile].astype(jnp.float32)
        put(lax.rem(rep + step, 8), mine.T)
        other = lax.rem(rep + 8 - step, 8)
        put(other, came[other].astype(jnp.float32))
    other = lax.rem(rep + 4, 8)
    mine = band[4 * tile :].astype(jnp.float32)
    theirs = came[other, : tile // 2].astype(jnp.float32)
    upper, lower = jnp.where(first, mine, theirs), jnp.where(first, theirs, mine)
    whole = jnp.concatenate([upper, lower], axis=0)
    put(other, jnp.where(first, whole.T, whole))


def finish(place, history, band, came):
    tile, order_full = band.shape[1], history.shape[1]
    return pl.pallas_call(
        finish_kernel,
        out_shape=like((tile, order_full)),
        grid_spec=pltpu.PrefetchScalarGridSpec(
            num_scalar_prefetch=1,
            grid=(1,),
            in_specs=[
                pl.BlockSpec((tile, order_full), lambda i, place: (place[0], 0)),
                pl.BlockSpec(band.shape, lambda i, place: (0, 0)),
                pl.BlockSpec(came.shape, lambda i, place: (0, 0, 0)),
            ],
            out_specs=pl.BlockSpec((tile, order_full), lambda i, place: (0, 0)),
        ),
        compiler_params=BIG,
    )(place, history, band, came)


def newton_kernel(table, stat, *refs):
    *cols, out, full = refs
    bands, shards, _, depth, tile = stat.shape
    order_full = bands * tile
    block = pl.program_id(0)
    squares = jnp.zeros((8, tile), jnp.float32)
    for band in range(bands):
        for shard in range(shards):
            part = stat[band, shard, 0].astype(jnp.float32)
            squares = squares + 2.0 * jnp.sum((part * part).reshape(-1, 8, tile), axis=0)
        part = stat[band, 0, 0, :tile].astype(jnp.float32)
        squares = squares - jnp.sum((part * part).reshape(-1, 8, tile), axis=0)
    frobenius = jnp.sqrt(jnp.sum(squares, keepdims=True)[:1, :1])
    norm_scale = math.sqrt(order_full) / (2.0 * frobenius)

    def at(index):
        return slice(index * tile, (index + 1) * tile)

    for band in range(bands):
        for part, row, step, inner, size in pieces(tile, shards):
            if step < 4:
                start, columns = (band + step) % bands * tile + inner, at(band)
            else:
                start = (band % 4 + 4) * tile + band // 4 * (tile // 2) + inner
                columns = at(band % 4)
            piece = stat[band, part, 0, row : row + size].astype(jnp.float32) * norm_scale
            full[start : start + size, columns] = piece.astype(jnp.bfloat16)
    for band in range(bands):
        for step in range(1, 5 if band < 4 else 4):
            other = (band + step) % bands
            full[at(band), at(other)] = full[at(other), at(band)].T

    row_ids = lax.broadcasted_iota(jnp.int32, (tile, tile), 0)
    col_ids = lax.broadcasted_iota(jnp.int32, (tile, tile), 1)
    diagonals = []
    for band in range(bands):
        corner = full[at(band), at(band)].astype(jnp.float32)
        values = jnp.sum(jnp.where(row_ids == col_ids, corner, 0.0), axis=0, keepdims=True)
        rounded = (1.5 - 0.5 * values).astype(jnp.bfloat16).astype(jnp.float32)
        diagonals.append(rounded + 0.5 * values)
    diagonal = jnp.concatenate(diagonals, axis=1)

    def times_scaled(left):
        return jnp.dot(left, full[...], preferred_element_type=jnp.float32)

    def times_factor(left):
        return left.astype(jnp.float32) * diagonal - 0.5 * times_scaled(left)

    first = table[REP_AT] * tile
    wide_rows = lax.broadcasted_iota(jnp.int32, (tile, order_full), 0) + first
    wide_cols = lax.broadcasted_iota(jnp.int32, (tile, order_full), 1)
    identity = jnp.where(wide_rows == wide_cols, 1.5, 0.0)
    mine = full[ds(first, tile, tile), :].astype(jnp.float32)
    mine = (identity - 0.5 * mine).astype(jnp.bfloat16)
    product = times_factor(times_scaled(mine).astype(jnp.bfloat16))
    update = (identity - 0.5 * product).astype(jnp.bfloat16)
    second = times_factor(update).astype(jnp.bfloat16)
    root = jnp.where(table[NEED_AT + block] >= ITERS, second, mine)
    for index, ref in enumerate(cols):

        @pl.when(block == index)
        def _(ref=ref):
            total = jnp.zeros(out.shape[1:], jnp.float32)
            for band in range(bands):
                total = total + jnp.dot(
                    root[:, at(band)], ref[band], preferred_element_type=jnp.float32
                )
            out[0] = total.astype(jnp.bfloat16)


def newton(table, stat, cols):
    bands, shards, home_count, depth, tile = stat.shape
    width = cols[0].shape[2]
    return pl.pallas_call(
        newton_kernel,
        out_shape=like((home_count, tile, width)),
        grid_spec=pltpu.PrefetchScalarGridSpec(
            num_scalar_prefetch=1,
            grid=(home_count,),
            in_specs=[
                pl.BlockSpec((bands, shards, 1, depth, tile), lambda i, table: (0, 0, i, 0, 0)),
            ]
            + [pl.BlockSpec((bands, tile, width), lambda i, table: (0, 0, 0))] * len(cols),
            out_specs=pl.BlockSpec((1, tile, width), lambda i, table: (i, 0, 0)),
            scratch_shapes=[pltpu.VMEM((bands * tile, bands * tile), jnp.bfloat16)],
        ),
        compiler_params=BIG,
    )(table, stat, *cols)


def exchange(array, axis):
    return lax.all_to_all(array, axis, split_axis=0, concat_axis=0, tiled=True)


def swap(parts, count):
    return [parts[0]] + [
        lax.ppermute(parts[step], "blk", [(i, (i + step) % count) for i in range(count)])
        for step in range(1, count)
    ]


def after(array, other):
    return lax.optimization_barrier((array, other))[0]


def body(partial_grads, owner_map, iterations, slot_history):
    owners = lax.axis_size("own")
    replicas = lax.axis_size("rep")
    shards = lax.axis_size("blk")
    my_rep, my_own, my_blk = lax.axis_index("rep"), lax.axis_index("own"), lax.axis_index("blk")
    _, home_count, order_full, band_cols = partial_grads.shape
    tile = order_full // replicas
    depth = (4 * tile + tile // 2) // shards
    total_blocks = owner_map.shape[0]
    history = slot_history[0, 0]
    place = jnp.stack([my_rep, my_blk]).astype(jnp.int32)

    position = jnp.arange(total_blocks, dtype=jnp.int32)
    same = owner_map[:, None] == owner_map[None, :]
    slot = jnp.sum(jnp.where(same & (position[None, :] < position[:, None]), 1, 0), axis=1)
    slot_ids = jnp.arange(shards, dtype=jnp.int32)
    held = (owner_map[None, :] == my_own) & (slot[None, :] == slot_ids[:, None])
    holder = jnp.sum(jnp.where(held, position[None, :] + 1, 0), axis=1) - 1
    my_owners = lax.dynamic_slice_in_dim(owner_map, my_own * home_count, home_count)
    my_need = lax.dynamic_slice_in_dim(iterations, my_own * home_count, home_count)
    table = jnp.concatenate([place, my_owners, my_need, holder]).astype(jnp.int32)

    outgoing = (
        partial_grads[0].reshape(home_count, replicas, tile, band_cols).transpose(1, 0, 2, 3)
    )
    history_arrived = swap(cut_history(place, history, shards, tile), shards)
    partials = exchange(outgoing, "rep")
    grad_tile = jnp.sum(partials.astype(jnp.float32), axis=0).astype(jnp.bfloat16)
    grad_cols = [lax.all_gather(grad_tile[0], "rep", axis=0, tiled=False)]
    for block in range(1, home_count):
        mine = after(grad_tile[block], grad_cols[-1])
        grad_cols.append(lax.all_gather(mine, "rep", axis=0, tiled=False))

    history_arrived = lax.optimization_barrier((tuple(history_arrived), grad_tile))[0]
    history_sent = call(spread_kernel, [table, *history_arrived], like((owners, depth, tile)))
    history_came = exchange(history_sent, "own")

    gram_parts = call(gram_kernel, [place, *grad_cols], like((shards, home_count, depth, tile)))
    gram, gram_sent = call(
        add_kernel,
        [table, exchange(after(gram_parts, history_came), "blk")],
        [like((home_count, depth, tile), jnp.float32), like((owners, depth, tile))],
    )
    stat = call(stat_kernel, [table, gram, history_came], like((home_count, depth, tile)))
    gram_came = exchange(after(gram_sent, history_came), "own")
    stat_band = lax.all_gather(stat, "blk", axis=0, tiled=False)
    stat_full = lax.all_gather(stat_band, "rep", axis=0, tiled=False)

    slot_parts = call(choose_kernel, [table, gram_came], like((shards, depth, tile)))
    band, turned = call(
        turn_kernel,
        [table, exchange(slot_parts, "blk")],
        [like((shards * depth, tile)), like((replicas, tile, tile))],
    )
    turned = exchange(turned, "rep")
    occupied = jnp.where(lax.dynamic_index_in_dim(holder, my_blk, 0, keepdims=False) >= 0, 1, 0)
    new_rows = finish(jnp.stack([my_rep, occupied]).astype(jnp.int32), history, band, turned)

    directions = newton(table, stat_full, grad_cols)
    return (directions, new_rows[None, None])


def solution(mesh):
    return jax.shard_map(
        body,
        mesh=mesh,
        in_specs=(P("rep", "own", None, "blk"), P(), P(), P("own", "blk", None, None)),
        out_specs=(P("own", "rep", "blk"), P("own", "blk", "rep", None)),
        check_vma=False,
    )
```

```python
import math

import jax
import jax.numpy as jnp
from jax import lax
from jax.experimental import pallas as pl
from jax.experimental.pallas import tpu as pltpu
from jax.sharding import Mesh, PartitionSpec as P

ITERS = 2


DECAY = 0.5
DAMPING = 0.05

REP = ("x", "core")
OWN = ("zl", "y")
BLK = "zh"
RING = ("zl", "zh")

BIG = pltpu.CompilerParams(vmem_limit_bytes=40 * 1024 * 1024)
SCALARS = pl.BlockSpec(memory_space=pltpu.SMEM)
WHOLE = pl.BlockSpec(memory_space=pltpu.VMEM)

BANDS, STEPS = 8, 5
REP_AT, BLK_AT, TURN_AT, NEED_AT, LEVEL_AT, HAS_AT, HISTORY_AT, GRAM_AT = 0, 1, 2, 4, 6, 7, 8, 24


def ds(start, size, unit):
    return pl.ds(pl.multiple_of(start, unit), size)


def like(shape, dtype=jnp.bfloat16):
    return jax.ShapeDtypeStruct(shape, dtype)


def call(kernel, ins, outs, in_specs=None, scratch=()):
    many = isinstance(outs, (list, tuple))
    return pl.pallas_call(
        kernel,
        out_shape=outs,
        in_specs=in_specs or [SCALARS] + [WHOLE] * (len(ins) - 1),
        out_specs=[WHOLE] * len(outs) if many else WHOLE,
        scratch_shapes=list(scratch),
        compiler_params=BIG,
    )(*ins)


def fan_kernel(table, grads, *outs):
    rows = outs[0].shape[1]
    for step, out in enumerate(outs):
        start = lax.rem(table[REP_AT] + step, BANDS) * rows
        for block in range(out.shape[0]):
            out[block] = grads[block, ds(start, rows, rows), :]


def sum_kernel(table, *refs):
    *ins, out = refs
    total = ins[0][...].astype(jnp.float32)
    for ref in ins[1:]:
        total = total + ref[...].astype(jnp.float32)
    out[...] = total.astype(jnp.bfloat16)


def history_kernel(table, column, out):
    tile = column.shape[1]
    shards = 4
    size = tile // shards
    for step in range(STEPS):
        start = lax.rem(table[REP_AT] + step, BANDS) * tile
        for shard in range(shards):
            piece = column[ds(start + shard * size, size, size), :]
            for level in range(out.shape[0] // shards):
                out[level * shards + shard, step * size : (step + 1) * size] = piece


def cut_history(table, history, places, tile, shards):
    order_full = history.shape[0]
    shape = (places, STEPS * tile // shards, tile)
    return pl.pallas_call(
        history_kernel,
        out_shape=like(shape),
        grid_spec=pltpu.PrefetchScalarGridSpec(
            num_scalar_prefetch=1,
            grid=(1,),
            in_specs=[pl.BlockSpec((order_full, tile), lambda i, table: (0, table[REP_AT]))],
            out_specs=pl.BlockSpec(shape, lambda i, table: (0, 0, 0)),
        ),
        compiler_params=BIG,
    )(table, history)


def take(table, tiles, first):
    def kernel(table, tiles, out):
        for place in range(out.shape[0]):
            out[place] = tiles[table[first + place]]

    return call(kernel, [table, tiles], like(tiles.shape))


def gram_kernel(table, band, *refs):
    *slices, out, sent = refs
    shards, home_count, tile, _ = band.shape
    size = tile // shards
    order_full = BANDS * tile
    start = table[BLK_AT] * size
    for block in range(home_count):
        total = jnp.zeros((STEPS * size, tile), jnp.float32)
        for shard in range(shards):
            left = [band[shard, block, ds(start, size, size), :]]
            left += [ref[shard, block] for ref in slices]
            total = total + lax.dot_general(
                jnp.concatenate(left, axis=0),
                band[shard, block],
                (((1,), (1,)), ((), ())),
                preferred_element_type=jnp.float32,
            )
        total = total * ((1.0 - DECAY) / order_full)
        out[block] = total
        for turn in range(sent.shape[0]):
            sent[turn, block] = total.astype(jnp.bfloat16)


def stat_kernel(table, gram, came, out):
    home_count, depth, tile = out.shape
    size = depth // STEPS
    row_ids = lax.broadcasted_iota(jnp.int32, (depth, tile), 0)
    col_ids = lax.broadcasted_iota(jnp.int32, (depth, tile), 1)
    on = (row_ids < size) & (row_ids + table[BLK_AT] * size == col_ids)
    damping = jnp.where(on, DAMPING, 0.0)
    for block in range(home_count):
        history = came[table[TURN_AT + block], block].astype(jnp.float32)
        out[block] = (DECAY * history + gram[block] + damping).astype(jnp.bfloat16)


def turn_kernel(table, came, band, sent):
    tile = sent.shape[1]
    size = came.shape[1] // STEPS
    shards = tile // size
    for shard in range(shards):
        part = came[table[LEVEL_AT] * shards + shard]
        for step in range(STEPS):
            start = step * tile + shard * size
            band[start : start + size] = part[step * size : (step + 1) * size]
    sent[...] = jnp.zeros_like(sent)
    for step in range(1, STEPS):
        sent[lax.rem(table[REP_AT] + step, BANDS)] = band[step * tile : (step + 1) * tile]


def finish_kernel(table, rows, band, came, out):
    tile = rows.shape[0]
    rep = table[REP_AT]

    def put(column, gram, damping=None):
        columns = ds(column * tile, tile, tile)
        history = rows[:, columns].astype(jnp.float32)
        fresh = DECAY * history + gram
        if damping is not None:
            fresh = fresh + damping
        out[:, columns] = jnp.where(table[HAS_AT] > 0, fresh, history).astype(jnp.bfloat16)

    row_ids = lax.broadcasted_iota(jnp.int32, (tile, tile), 0)
    col_ids = lax.broadcasted_iota(jnp.int32, (tile, tile), 1)
    put(rep, band[:tile].astype(jnp.float32), jnp.where(row_ids == col_ids, DAMPING, 0.0))
    for step in range(1, STEPS):
        other = lax.rem(rep + BANDS - step, BANDS)
        put(other, came[other].astype(jnp.float32))
        if step < STEPS - 1:
            mine = band[step * tile : (step + 1) * tile].astype(jnp.float32)
            put(lax.rem(rep + step, BANDS), mine.T)


def finish(table, history, band, came):
    tile, order_full = band.shape[1], history.shape[1]
    return pl.pallas_call(
        finish_kernel,
        out_shape=like((tile, order_full)),
        grid_spec=pltpu.PrefetchScalarGridSpec(
            num_scalar_prefetch=1,
            grid=(1,),
            in_specs=[
                pl.BlockSpec((tile, order_full), lambda i, table: (table[REP_AT], 0)),
                pl.BlockSpec(band.shape, lambda i, table: (0, 0)),
                pl.BlockSpec(came.shape, lambda i, table: (0, 0, 0)),
            ],
            out_specs=pl.BlockSpec((tile, order_full), lambda i, table: (0, 0)),
        ),
        compiler_params=BIG,
    )(table, history, band, came)


def newton_kernel(table, stat, cols, out, full):
    bands, shards, _, depth, tile = stat.shape
    size = depth // STEPS
    order_full = bands * tile
    block = pl.program_id(0)
    squares = jnp.zeros((8, tile), jnp.float32)
    for band in range(bands):
        for shard in range(shards):
            part = stat[band, shard, 0].astype(jnp.float32)
            part = (part * part).reshape(-1, 8, tile)
            ends, middle = size // 8, (STEPS - 1) * size // 8
            squares = squares + jnp.sum(part, axis=0) + jnp.sum(part[ends:middle], axis=0)
    frobenius = jnp.sqrt(jnp.sum(squares, keepdims=True)[:1, :1])
    norm_scale = math.sqrt(order_full) / (2.0 * frobenius)

    def at(index):
        return slice(index * tile, (index + 1) * tile)

    for band in range(bands):
        for shard in range(shards):
            part = (stat[band, shard, 0].astype(jnp.float32) * norm_scale).astype(jnp.bfloat16)
            for step in range(STEPS):
                start = (band + step) % bands * tile + shard * size
                full[start : start + size, at(band)] = part[step * size : (step + 1) * size]
    for band in range(bands):
        for step in range(1, STEPS - 1):
            other = (band + step) % bands
            full[at(band), at(other)] = full[at(other), at(band)].T

    row_ids = lax.broadcasted_iota(jnp.int32, (tile, tile), 0)
    col_ids = lax.broadcasted_iota(jnp.int32, (tile, tile), 1)
    diagonals = []
    for band in range(bands):
        corner = full[at(band), at(band)].astype(jnp.float32)
        values = jnp.sum(jnp.where(row_ids == col_ids, corner, 0.0), axis=0, keepdims=True)
        rounded = (1.5 - 0.5 * values).astype(jnp.bfloat16).astype(jnp.float32)
        diagonals.append(rounded + 0.5 * values)
    diagonal = jnp.concatenate(diagonals, axis=1)

    def times_scaled(left):
        return jnp.dot(left, full[...], preferred_element_type=jnp.float32)

    def times_factor(left):
        return left.astype(jnp.float32) * diagonal - 0.5 * times_scaled(left)

    first = table[REP_AT] * tile
    wide_rows = lax.broadcasted_iota(jnp.int32, (tile, order_full), 0) + first
    wide_cols = lax.broadcasted_iota(jnp.int32, (tile, order_full), 1)
    identity = jnp.where(wide_rows == wide_cols, 1.5, 0.0)
    mine = full[ds(first, tile, tile), :].astype(jnp.float32)
    mine = (identity - 0.5 * mine).astype(jnp.bfloat16)
    product = times_factor(times_scaled(mine).astype(jnp.bfloat16))
    update = (identity - 0.5 * product).astype(jnp.bfloat16)
    second = times_factor(update).astype(jnp.bfloat16)
    root = jnp.where(table[NEED_AT + block] >= ITERS, second, mine)
    total = jnp.zeros(out.shape[1:], jnp.float32)
    for band in range(bands):
        total = total + jnp.dot(root[:, at(band)], cols[band, 0], preferred_element_type=jnp.float32)
    out[0] = total.astype(jnp.bfloat16)


def newton(table, stat, cols):
    bands, shards, home_count, depth, tile = stat.shape
    width = cols.shape[3]
    return pl.pallas_call(
        newton_kernel,
        out_shape=like((home_count, tile, width)),
        grid_spec=pltpu.PrefetchScalarGridSpec(
            num_scalar_prefetch=1,
            grid=(home_count,),
            in_specs=[
                pl.BlockSpec((bands, shards, 1, depth, tile), lambda i, table: (0, 0, i, 0, 0)),
                pl.BlockSpec((bands, 1, tile, width), lambda i, table: (0, i, 0, 0)),
            ],
            out_specs=pl.BlockSpec((1, tile, width), lambda i, table: (i, 0, 0)),
            scratch_shapes=[pltpu.VMEM((bands * tile, bands * tile), jnp.bfloat16)],
        ),
        compiler_params=BIG,
    )(table, stat, cols)


def exchange(array, axis):
    return lax.all_to_all(array, axis, split_axis=0, concat_axis=0, tiled=True)


def shift(array, step):
    return lax.ppermute(array, REP, [(i, (i + step) % BANDS) for i in range(BANDS)])


def after(array, other):
    return lax.optimization_barrier((array, other))[0]


def tables(owner_map, iterations, home_count):
    levels, turns, shards = lax.axis_size("zl"), lax.axis_size("y"), lax.axis_size(BLK)
    my_level, my_turn, my_blk = lax.axis_index("zl"), lax.axis_index("y"), lax.axis_index(BLK)
    my_own = lax.axis_index(OWN)
    total_blocks = owner_map.shape[0]
    column = turns * home_count
    position = jnp.arange(total_blocks, dtype=jnp.int32)
    same = owner_map[:, None] == owner_map[None, :]
    slot = jnp.sum(jnp.where(same & (position[None, :] < position[:, None]), 1, 0), axis=1)
    place_ids = jnp.arange(levels * turns * shards, dtype=jnp.int32)
    lands = (owner_map * shards + slot)[None, :] == place_ids[:, None]
    holder = jnp.sum(jnp.where(lands, position[None, :] + 1, 0), axis=1) - 1
    holder = holder.reshape(levels, turns, shards)
    mine = holder[my_level, my_turn, my_blk]
    from_ring = (owner_map // turns) * shards + slot
    cut = lax.dynamic_slice_in_dim
    return jnp.concatenate(
        [
            jnp.stack([lax.axis_index(REP), my_blk]),
            cut(owner_map, my_own * home_count, home_count) % turns,
            cut(iterations, my_own * home_count, home_count),
            jnp.stack([jnp.maximum(mine, 0) // column, jnp.where(mine >= 0, 1, 0)]),
            cut(from_ring, my_level * column, column),
            (jnp.maximum(holder, 0) % column)[:, my_turn].reshape(-1),
        ]
    ).astype(jnp.int32)


def body(partial_grads, owner_map, iterations, slot_history):
    turns, shards = lax.axis_size("y"), lax.axis_size(BLK)
    ring = lax.axis_size("zl") * shards
    my_blk = lax.axis_index(BLK)
    _, home_count, order_full, width = partial_grads.shape
    tile = order_full // BANDS
    size = tile // shards
    depth = STEPS * size
    history = slot_history[0, 0]
    table = tables(owner_map, iterations, home_count)
    place = jnp.stack([lax.axis_index(REP), my_blk]).astype(jnp.int32)

    history_ring = exchange(cut_history(place, history, ring, tile, shards), RING)

    partials = call(
        fan_kernel, [place, partial_grads[0]], [like((home_count, tile, width))] * BANDS
    )
    partials = [partials[0]] + [shift(partials[step], step) for step in range(1, BANDS)]
    grad_tile = call(sum_kernel, [place, *partials], like((home_count, tile, width)))
    grad_cols = lax.all_gather(grad_tile, REP, axis=0, tiled=False)

    history_sent = take(table, history_ring, HISTORY_AT)
    history_sent = history_sent.reshape(turns, home_count, depth, tile)
    history_came = exchange(history_sent, "y")

    grad_band = lax.all_gather(grad_tile, BLK, axis=0, tiled=False)
    mine = lax.dynamic_slice_in_dim(grad_band, my_blk * size, size, 2)
    slices = [shift(mine, -step) for step in range(1, STEPS)]
    gram, gram_sent = call(
        gram_kernel,
        [place, grad_band, *slices],
        [like((home_count, depth, tile), jnp.float32), like((turns, home_count, depth, tile))],
    )
    gram_came = exchange(after(gram_sent, history_came), "y")
    stat = call(stat_kernel, [table, gram, history_came], like((home_count, depth, tile)))
    stat_band = lax.all_gather(stat, BLK, axis=0, tiled=False)
    stat_full = lax.all_gather(stat_band, REP, axis=0, tiled=False)

    gram_sent = take(table, gram_came.reshape(ring, depth, tile), GRAM_AT)
    gram_slot = exchange(gram_sent, RING)
    band, turned = call(
        turn_kernel, [table, gram_slot], [like((STEPS * tile, tile)), like((BANDS, tile, tile))]
    )
    new_rows = finish(table, history, band, exchange(turned, REP))

    directions = newton(table, stat_full, grad_cols)
    return (directions, new_rows[None, None])


def solution(mesh):
    fine = Mesh(mesh.devices.reshape(4, 2, 4, 8, 4), ("x", "core", "zl", "y", "zh"))
    return jax.shard_map(
        body,
        mesh=fine,
        in_specs=(P(REP, OWN, None, BLK), P(), P(), P(OWN, BLK, None, None)),
        out_specs=(P(OWN, REP, BLK), P(OWN, BLK, REP, None)),
        check_vma=False,
    )
```

```python
import math

import jax
import jax.numpy as jnp
from jax import lax
from jax.experimental import pallas as pl
from jax.experimental.pallas import tpu as pltpu
from jax.sharding import Mesh, PartitionSpec as P

ITERS = 2


DECAY = 0.5
DAMPING = 0.05

REP = ("x", "core")
OWN = ("zl", "y")
BLK = "zh"
RING = ("zl", "zh")

BIG = pltpu.CompilerParams(vmem_limit_bytes=40 * 1024 * 1024)
SCALARS = pl.BlockSpec(memory_space=pltpu.SMEM)
WHOLE = pl.BlockSpec(memory_space=pltpu.VMEM)

BANDS, STEPS = 8, 5
REP_AT, BLK_AT, TURN_AT, NEED_AT, LEVEL_AT, HAS_AT, HISTORY_AT, GRAM_AT = 0, 1, 2, 4, 6, 10, 11, 27


def ds(start, size, unit):
    return pl.ds(pl.multiple_of(start, unit), size)


def like(shape, dtype=jnp.bfloat16):
    return jax.ShapeDtypeStruct(shape, dtype)


def call(kernel, ins, outs, in_specs=None, scratch=()):
    many = isinstance(outs, (list, tuple))
    return pl.pallas_call(
        kernel,
        out_shape=outs,
        in_specs=in_specs or [SCALARS] + [WHOLE] * (len(ins) - 1),
        out_specs=[WHOLE] * len(outs) if many else WHOLE,
        scratch_shapes=list(scratch),
        compiler_params=BIG,
    )(*ins)


def fan_kernel(table, grads, *outs):
    rows = outs[0].shape[1]
    for step, out in enumerate(outs):
        start = lax.rem(table[REP_AT] + step, BANDS) * rows
        for block in range(out.shape[0]):
            out[block] = grads[block, ds(start, rows, rows), :]


def sum_kernel(table, *refs):
    *ins, out = refs
    total = ins[0][...].astype(jnp.float32)
    for ref in ins[1:]:
        total = total + ref[...].astype(jnp.float32)
    out[...] = total.astype(jnp.bfloat16)


def history_kernel(table, column, out):
    tile = column.shape[1]
    shards = 4
    size = tile // shards
    for step in range(STEPS):
        start = lax.rem(table[REP_AT] + step, BANDS) * tile
        for shard in range(shards):
            piece = column[ds(start + shard * size, size, size), :]
            for level in range(out.shape[0] // shards):
                out[level * shards + shard, step * size : (step + 1) * size] = piece


def cut_history(table, history, places, tile, shards):
    order_full = history.shape[0]
    shape = (places, STEPS * tile // shards, tile)
    return pl.pallas_call(
        history_kernel,
        out_shape=like(shape),
        grid_spec=pltpu.PrefetchScalarGridSpec(
            num_scalar_prefetch=1,
            grid=(1,),
            in_specs=[pl.BlockSpec((order_full, tile), lambda i, table: (0, table[REP_AT]))],
            out_specs=pl.BlockSpec(shape, lambda i, table: (0, 0, 0)),
        ),
        compiler_params=BIG,
    )(table, history)


def take(table, tiles, first):
    def kernel(table, tiles, out):
        for place in range(out.shape[0]):
            out[place] = tiles[table[first + place]]

    return call(kernel, [table, tiles], like(tiles.shape))


def gram_kernel(table, band, *refs):
    *slices, out, sent = refs
    shards, home_count, tile, _ = band.shape
    size = tile // shards
    order_full = BANDS * tile
    start = table[BLK_AT] * size
    for block in range(home_count):
        total = jnp.zeros((STEPS * size, tile), jnp.float32)
        for shard in range(shards):
            left = [band[shard, block, ds(start, size, size), :]]
            left += [ref[shard, block] for ref in slices]
            total = total + lax.dot_general(
                jnp.concatenate(left, axis=0),
                band[shard, block],
                (((1,), (1,)), ((), ())),
                preferred_element_type=jnp.float32,
            )
        total = total * ((1.0 - DECAY) / order_full)
        out[block] = total
        sent[block] = total.astype(jnp.bfloat16)


def stat_kernel(table, gram, came, out):
    home_count, depth, tile = out.shape
    size = depth // STEPS
    row_ids = lax.broadcasted_iota(jnp.int32, (depth, tile), 0)
    col_ids = lax.broadcasted_iota(jnp.int32, (depth, tile), 1)
    on = (row_ids < size) & (row_ids + table[BLK_AT] * size == col_ids)
    damping = jnp.where(on, DAMPING, 0.0)
    for block in range(home_count):
        history = came[table[TURN_AT + block], block].astype(jnp.float32)
        out[block] = (DECAY * history + gram[block] + damping).astype(jnp.bfloat16)


def choose_kernel(table, came, out):
    shards = out.shape[0]
    for shard in range(shards):
        out[shard] = came[table[LEVEL_AT + shard] * shards + shard]


def turn_kernel(table, came, band, sent):
    tile = sent.shape[1]
    size = came.shape[1] // STEPS
    shards = tile // size
    for shard in range(shards):
        part = came[shard]
        for step in range(STEPS):
            start = step * tile + shard * size
            band[start : start + size] = part[step * size : (step + 1) * size]
    sent[...] = jnp.zeros_like(sent)
    for step in range(1, STEPS):
        sent[lax.rem(table[REP_AT] + step, BANDS)] = band[step * tile : (step + 1) * tile]


def finish_kernel(table, rows, band, came, out):
    tile = rows.shape[0]
    rep = table[REP_AT]

    def put(column, gram, damping=None):
        columns = ds(column * tile, tile, tile)
        history = rows[:, columns].astype(jnp.float32)
        fresh = DECAY * history + gram
        if damping is not None:
            fresh = fresh + damping
        out[:, columns] = jnp.where(table[HAS_AT] > 0, fresh, history).astype(jnp.bfloat16)

    row_ids = lax.broadcasted_iota(jnp.int32, (tile, tile), 0)
    col_ids = lax.broadcasted_iota(jnp.int32, (tile, tile), 1)
    put(rep, band[:tile].astype(jnp.float32), jnp.where(row_ids == col_ids, DAMPING, 0.0))
    for step in range(1, STEPS):
        other = lax.rem(rep + BANDS - step, BANDS)
        put(other, came[other].astype(jnp.float32))
        if step < STEPS - 1:
            mine = band[step * tile : (step + 1) * tile].astype(jnp.float32)
            put(lax.rem(rep + step, BANDS), mine.T)


def finish(table, history, band, came):
    tile, order_full = band.shape[1], history.shape[1]
    return pl.pallas_call(
        finish_kernel,
        out_shape=like((tile, order_full)),
        grid_spec=pltpu.PrefetchScalarGridSpec(
            num_scalar_prefetch=1,
            grid=(1,),
            in_specs=[
                pl.BlockSpec((tile, order_full), lambda i, table: (table[REP_AT], 0)),
                pl.BlockSpec(band.shape, lambda i, table: (0, 0)),
                pl.BlockSpec(came.shape, lambda i, table: (0, 0, 0)),
            ],
            out_specs=pl.BlockSpec((tile, order_full), lambda i, table: (0, 0)),
        ),
        compiler_params=BIG,
    )(table, history, band, came)


def newton_kernel(table, stat, cols, out, full):
    bands, shards, _, depth, tile = stat.shape
    size = depth // STEPS
    order_full = bands * tile
    block = pl.program_id(0)
    squares = jnp.zeros((8, tile), jnp.float32)
    for band in range(bands):
        for shard in range(shards):
            part = stat[band, shard, 0].astype(jnp.float32)
            part = (part * part).reshape(-1, 8, tile)
            ends, middle = size // 8, (STEPS - 1) * size // 8
            squares = squares + jnp.sum(part, axis=0) + jnp.sum(part[ends:middle], axis=0)
    frobenius = jnp.sqrt(jnp.sum(squares, keepdims=True)[:1, :1])
    norm_scale = math.sqrt(order_full) / (2.0 * frobenius)

    def at(index):
        return slice(index * tile, (index + 1) * tile)

    for band in range(bands):
        for shard in range(shards):
            part = (stat[band, shard, 0].astype(jnp.float32) * norm_scale).astype(jnp.bfloat16)
            for step in range(STEPS):
                start = (band + step) % bands * tile + shard * size
                full[start : start + size, at(band)] = part[step * size : (step + 1) * size]
    for band in range(bands):
        for step in range(1, STEPS - 1):
            other = (band + step) % bands
            full[at(band), at(other)] = full[at(other), at(band)].T

    row_ids = lax.broadcasted_iota(jnp.int32, (tile, tile), 0)
    col_ids = lax.broadcasted_iota(jnp.int32, (tile, tile), 1)
    diagonals = []
    for band in range(bands):
        corner = full[at(band), at(band)].astype(jnp.float32)
        values = jnp.sum(jnp.where(row_ids == col_ids, corner, 0.0), axis=0, keepdims=True)
        rounded = (1.5 - 0.5 * values).astype(jnp.bfloat16).astype(jnp.float32)
        diagonals.append(rounded + 0.5 * values)
    diagonal = jnp.concatenate(diagonals, axis=1)

    def times_scaled(left):
        return jnp.dot(left, full[...], preferred_element_type=jnp.float32)

    def times_factor(left):
        return left.astype(jnp.float32) * diagonal - 0.5 * times_scaled(left)

    first = table[REP_AT] * tile
    wide_rows = lax.broadcasted_iota(jnp.int32, (tile, order_full), 0) + first
    wide_cols = lax.broadcasted_iota(jnp.int32, (tile, order_full), 1)
    identity = jnp.where(wide_rows == wide_cols, 1.5, 0.0)
    mine = full[ds(first, tile, tile), :].astype(jnp.float32)
    mine = (identity - 0.5 * mine).astype(jnp.bfloat16)
    product = times_factor(times_scaled(mine).astype(jnp.bfloat16))
    update = (identity - 0.5 * product).astype(jnp.bfloat16)
    second = times_factor(update).astype(jnp.bfloat16)
    root = jnp.where(table[NEED_AT + block] >= ITERS, second, mine)
    total = jnp.zeros(out.shape[1:], jnp.float32)
    for band in range(bands):
        total = total + jnp.dot(root[:, at(band)], cols[band, 0], preferred_element_type=jnp.float32)
    out[0] = total.astype(jnp.bfloat16)


def newton(table, stat, cols):
    bands, shards, home_count, depth, tile = stat.shape
    width = cols.shape[3]
    return pl.pallas_call(
        newton_kernel,
        out_shape=like((home_count, tile, width)),
        grid_spec=pltpu.PrefetchScalarGridSpec(
            num_scalar_prefetch=1,
            grid=(home_count,),
            in_specs=[
                pl.BlockSpec((bands, shards, 1, depth, tile), lambda i, table: (0, 0, i, 0, 0)),
                pl.BlockSpec((bands, 1, tile, width), lambda i, table: (0, i, 0, 0)),
            ],
            out_specs=pl.BlockSpec((1, tile, width), lambda i, table: (i, 0, 0)),
            scratch_shapes=[pltpu.VMEM((bands * tile, bands * tile), jnp.bfloat16)],
        ),
        compiler_params=BIG,
    )(table, stat, cols)


def exchange(array, axis):
    return lax.all_to_all(array, axis, split_axis=0, concat_axis=0, tiled=True)


def shift(array, step):
    return lax.ppermute(array, REP, [(i, (i + step) % BANDS) for i in range(BANDS)])


def after(array, other):
    return lax.optimization_barrier((array, other))[0]


def tables(owner_map, iterations, home_count):
    levels, turns, shards = lax.axis_size("zl"), lax.axis_size("y"), lax.axis_size(BLK)
    my_level, my_turn, my_blk = lax.axis_index("zl"), lax.axis_index("y"), lax.axis_index(BLK)
    my_own = lax.axis_index(OWN)
    total_blocks = owner_map.shape[0]
    column = turns * home_count
    position = jnp.arange(total_blocks, dtype=jnp.int32)
    same = owner_map[:, None] == owner_map[None, :]
    slot = jnp.sum(jnp.where(same & (position[None, :] < position[:, None]), 1, 0), axis=1)
    place_ids = jnp.arange(levels * turns * shards, dtype=jnp.int32)
    lands = (owner_map * shards + slot)[None, :] == place_ids[:, None]
    holder = jnp.sum(jnp.where(lands, position[None, :] + 1, 0), axis=1) - 1
    holder = holder.reshape(levels, turns, shards)
    mine = holder[my_level, my_turn, my_blk]
    from_ring = (owner_map // turns) * shards + slot
    cut = lax.dynamic_slice_in_dim
    return jnp.concatenate(
        [
            jnp.stack([lax.axis_index(REP), my_blk]),
            cut(owner_map, my_own * home_count, home_count) % turns,
            cut(iterations, my_own * home_count, home_count),
            jnp.maximum(holder, 0)[my_level, my_turn] // column,
            jnp.where(mine >= 0, 1, 0)[None],
            cut(from_ring, my_level * column, column),
            (jnp.maximum(holder, 0) % column)[:, my_turn].reshape(-1),
        ]
    ).astype(jnp.int32)


def body(partial_grads, owner_map, iterations, slot_history):
    turns, shards = lax.axis_size("y"), lax.axis_size(BLK)
    ring = lax.axis_size("zl") * shards
    my_blk = lax.axis_index(BLK)
    _, home_count, order_full, width = partial_grads.shape
    tile = order_full // BANDS
    size = tile // shards
    depth = STEPS * size
    history = slot_history[0, 0]
    table = tables(owner_map, iterations, home_count)
    place = jnp.stack([lax.axis_index(REP), my_blk]).astype(jnp.int32)

    history_ring = exchange(cut_history(place, history, ring, tile, shards), RING)

    partials = call(
        fan_kernel, [place, partial_grads[0]], [like((home_count, tile, width))] * BANDS
    )
    partials = [partials[0]] + [shift(partials[step], step) for step in range(1, BANDS)]
    grad_tile = call(sum_kernel, [place, *partials], like((home_count, tile, width)))
    grad_cols = lax.all_gather(grad_tile, REP, axis=0, tiled=False)

    grad_band = lax.all_gather(grad_tile, BLK, axis=0, tiled=False)

    history_sent = take(table, after(history_ring, grad_band), HISTORY_AT)
    history_sent = history_sent.reshape(turns, home_count, depth, tile)
    history_came = exchange(history_sent, "y")

    mine = lax.dynamic_slice_in_dim(grad_band, my_blk * size, size, 2)
    slices = [shift(mine, -step) for step in range(1, STEPS)]
    gram, gram_sent = call(
        gram_kernel,
        [place, grad_band, *slices],
        [like((home_count, depth, tile), jnp.float32), like((home_count, depth, tile))],
    )
    stat = call(stat_kernel, [table, gram, history_came], like((home_count, depth, tile)))
    stat_band = lax.all_gather(stat, BLK, axis=0, tiled=False)
    stat_full = lax.all_gather(stat_band, REP, axis=0, tiled=False)

    gram_came = lax.all_gather(after(gram_sent, stat_band), "y", axis=0, tiled=False)
    gram_sent = take(table, gram_came.reshape(ring, depth, tile), GRAM_AT)
    gram_level = exchange(gram_sent, "zl")
    gram_slot = call(choose_kernel, [table, gram_level], like((shards, depth, tile)))
    gram_slot = exchange(gram_slot, BLK)
    band, turned = call(
        turn_kernel,
        [table, gram_slot],
        [like((STEPS * tile, tile)), like((BANDS, tile, tile))],
    )
    directions = newton(table, stat_full, grad_cols)
    turned = after(exchange(turned, REP), directions)
    new_rows = finish(table, history, band, turned)
    return (directions, new_rows[None, None])


def solution(mesh):
    fine = Mesh(mesh.devices.reshape(4, 2, 4, 8, 4), ("x", "core", "zl", "y", "zh"))
    return jax.shard_map(
        body,
        mesh=fine,
        in_specs=(P(REP, OWN, None, BLK), P(), P(), P(OWN, BLK, None, None)),
        out_specs=(P(OWN, REP, BLK), P(OWN, BLK, REP, None)),
        check_vma=False,
    )
```

```python
import math

import jax
import jax.numpy as jnp
from jax import lax
from jax.experimental import pallas as pl
from jax.experimental.pallas import tpu as pltpu
from jax.sharding import Mesh, PartitionSpec as P

ITERS = 2


DECAY = 0.5
DAMPING = 0.05

REP = ("x", "core")
OWN = ("zl", "y")
BLK = "zh"
RING = ("zl", "zh")

BIG = pltpu.CompilerParams(vmem_limit_bytes=40 * 1024 * 1024)
SCALARS = pl.BlockSpec(memory_space=pltpu.SMEM)
WHOLE = pl.BlockSpec(memory_space=pltpu.VMEM)

BANDS, STEPS = 8, 5
REP_AT, BLK_AT, TURN_AT, NEED_AT, LEVEL_AT, HAS_AT, HISTORY_AT, GRAM_AT = 0, 1, 2, 4, 6, 10, 11, 27


def ds(start, size, unit):
    return pl.ds(pl.multiple_of(start, unit), size)


def like(shape, dtype=jnp.bfloat16):
    return jax.ShapeDtypeStruct(shape, dtype)


def call(kernel, ins, outs, in_specs=None, scratch=()):
    many = isinstance(outs, (list, tuple))
    return pl.pallas_call(
        kernel,
        out_shape=outs,
        in_specs=in_specs or [SCALARS] + [WHOLE] * (len(ins) - 1),
        out_specs=[WHOLE] * len(outs) if many else WHOLE,
        scratch_shapes=list(scratch),
        compiler_params=BIG,
    )(*ins)


def fan_kernel(table, grads, *outs):
    rows = outs[0].shape[1]
    for step, out in enumerate(outs):
        start = lax.rem(table[REP_AT] + step, BANDS) * rows
        for block in range(out.shape[0]):
            out[block] = grads[block, ds(start, rows, rows), :]


def sum_kernel(table, *refs):
    *ins, out = refs
    total = ins[0][...].astype(jnp.float32)
    for ref in ins[1:]:
        total = total + ref[...].astype(jnp.float32)
    out[...] = total.astype(jnp.bfloat16)


def history_kernel(table, column, out):
    tile = column.shape[1]
    shards = 4
    size = tile // shards
    for step in range(STEPS):
        start = lax.rem(table[REP_AT] + step, BANDS) * tile
        for shard in range(shards):
            piece = column[ds(start + shard * size, size, size), :]
            for level in range(out.shape[0] // shards):
                out[level * shards + shard, step * size : (step + 1) * size] = piece


def cut_history(table, history, places, tile, shards):
    order_full = history.shape[0]
    shape = (places, STEPS * tile // shards, tile)
    return pl.pallas_call(
        history_kernel,
        out_shape=like(shape),
        grid_spec=pltpu.PrefetchScalarGridSpec(
            num_scalar_prefetch=1,
            grid=(1,),
            in_specs=[pl.BlockSpec((order_full, tile), lambda i, table: (0, table[REP_AT]))],
            out_specs=pl.BlockSpec(shape, lambda i, table: (0, 0, 0)),
        ),
        compiler_params=BIG,
    )(table, history)


def take(table, tiles, first):
    def kernel(table, tiles, out):
        for place in range(out.shape[0]):
            out[place] = tiles[table[first + place]]

    return call(kernel, [table, tiles], like(tiles.shape))


def gram_kernel(table, band, *refs):
    *slices, out, sent = refs
    shards, home_count, tile, _ = band.shape
    size = tile // shards
    order_full = BANDS * tile
    start = table[BLK_AT] * size
    for block in range(home_count):
        total = jnp.zeros((STEPS * size, tile), jnp.float32)
        for shard in range(shards):
            left = [band[shard, block, ds(start, size, size), :]]
            left += [ref[shard, block] for ref in slices]
            total = total + lax.dot_general(
                jnp.concatenate(left, axis=0),
                band[shard, block],
                (((1,), (1,)), ((), ())),
                preferred_element_type=jnp.float32,
            )
        total = total * ((1.0 - DECAY) / order_full)
        out[block] = total
        for turn in range(sent.shape[0]):
            sent[turn, block] = total.astype(jnp.bfloat16)


def stat_kernel(table, gram, came, out):
    home_count, depth, tile = out.shape
    size = depth // STEPS
    row_ids = lax.broadcasted_iota(jnp.int32, (depth, tile), 0)
    col_ids = lax.broadcasted_iota(jnp.int32, (depth, tile), 1)
    on = (row_ids < size) & (row_ids + table[BLK_AT] * size == col_ids)
    damping = jnp.where(on, DAMPING, 0.0)
    for block in range(home_count):
        history = came[table[TURN_AT + block], block].astype(jnp.float32)
        out[block] = (DECAY * history + gram[block] + damping).astype(jnp.bfloat16)


def choose_kernel(table, came, out):
    shards = out.shape[0]
    for shard in range(shards):
        out[shard] = came[table[LEVEL_AT + shard] * shards + shard]


def turn_kernel(table, came, band, sent):
    tile = sent.shape[1]
    size = came.shape[1] // STEPS
    shards = tile // size
    for shard in range(shards):
        part = came[shard]
        for step in range(STEPS):
            start = step * tile + shard * size
            band[start : start + size] = part[step * size : (step + 1) * size]
    sent[...] = jnp.zeros_like(sent)
    for step in range(1, STEPS):
        sent[lax.rem(table[REP_AT] + step, BANDS)] = band[step * tile : (step + 1) * tile]


def finish_kernel(table, rows, band, came, out):
    tile = rows.shape[0]
    rep = table[REP_AT]

    def put(column, gram, damping=None):
        columns = ds(column * tile, tile, tile)
        history = rows[:, columns].astype(jnp.float32)
        fresh = DECAY * history + gram
        if damping is not None:
            fresh = fresh + damping
        out[:, columns] = jnp.where(table[HAS_AT] > 0, fresh, history).astype(jnp.bfloat16)

    row_ids = lax.broadcasted_iota(jnp.int32, (tile, tile), 0)
    col_ids = lax.broadcasted_iota(jnp.int32, (tile, tile), 1)
    put(rep, band[:tile].astype(jnp.float32), jnp.where(row_ids == col_ids, DAMPING, 0.0))
    for step in range(1, STEPS):
        other = lax.rem(rep + BANDS - step, BANDS)
        put(other, came[other].astype(jnp.float32))
        if step < STEPS - 1:
            mine = band[step * tile : (step + 1) * tile].astype(jnp.float32)
            put(lax.rem(rep + step, BANDS), mine.T)


def finish(table, history, band, came):
    tile, order_full = band.shape[1], history.shape[1]
    return pl.pallas_call(
        finish_kernel,
        out_shape=like((tile, order_full)),
        grid_spec=pltpu.PrefetchScalarGridSpec(
            num_scalar_prefetch=1,
            grid=(1,),
            in_specs=[
                pl.BlockSpec((tile, order_full), lambda i, table: (table[REP_AT], 0)),
                pl.BlockSpec(band.shape, lambda i, table: (0, 0)),
                pl.BlockSpec(came.shape, lambda i, table: (0, 0, 0)),
            ],
            out_specs=pl.BlockSpec((tile, order_full), lambda i, table: (0, 0)),
        ),
        compiler_params=BIG,
    )(table, history, band, came)


def newton_kernel(table, stat, cols, out, full):
    bands, shards, _, depth, tile = stat.shape
    size = depth // STEPS
    order_full = bands * tile
    block = pl.program_id(0)
    squares = jnp.zeros((8, tile), jnp.float32)
    for band in range(bands):
        for shard in range(shards):
            part = stat[band, shard, 0].astype(jnp.float32)
            part = (part * part).reshape(-1, 8, tile)
            ends, middle = size // 8, (STEPS - 1) * size // 8
            squares = squares + jnp.sum(part, axis=0) + jnp.sum(part[ends:middle], axis=0)
    frobenius = jnp.sqrt(jnp.sum(squares, keepdims=True)[:1, :1])
    norm_scale = math.sqrt(order_full) / (2.0 * frobenius)

    def at(index):
        return slice(index * tile, (index + 1) * tile)

    for band in range(bands):
        for shard in range(shards):
            part = (stat[band, shard, 0].astype(jnp.float32) * norm_scale).astype(jnp.bfloat16)
            for step in range(STEPS):
                start = (band + step) % bands * tile + shard * size
                full[start : start + size, at(band)] = part[step * size : (step + 1) * size]
    for band in range(bands):
        for step in range(1, STEPS - 1):
            other = (band + step) % bands
            full[at(band), at(other)] = full[at(other), at(band)].T

    row_ids = lax.broadcasted_iota(jnp.int32, (tile, tile), 0)
    col_ids = lax.broadcasted_iota(jnp.int32, (tile, tile), 1)
    diagonals = []
    for band in range(bands):
        corner = full[at(band), at(band)].astype(jnp.float32)
        values = jnp.sum(jnp.where(row_ids == col_ids, corner, 0.0), axis=0, keepdims=True)
        rounded = (1.5 - 0.5 * values).astype(jnp.bfloat16).astype(jnp.float32)
        diagonals.append(rounded + 0.5 * values)
    diagonal = jnp.concatenate(diagonals, axis=1)

    def times_scaled(left):
        return jnp.dot(left, full[...], preferred_element_type=jnp.float32)

    def times_factor(left):
        return left.astype(jnp.float32) * diagonal - 0.5 * times_scaled(left)

    first = table[REP_AT] * tile
    wide_rows = lax.broadcasted_iota(jnp.int32, (tile, order_full), 0) + first
    wide_cols = lax.broadcasted_iota(jnp.int32, (tile, order_full), 1)
    identity = jnp.where(wide_rows == wide_cols, 1.5, 0.0)
    mine = full[ds(first, tile, tile), :].astype(jnp.float32)
    mine = (identity - 0.5 * mine).astype(jnp.bfloat16)
    product = times_factor(times_scaled(mine).astype(jnp.bfloat16))
    update = (identity - 0.5 * product).astype(jnp.bfloat16)
    second = times_factor(update).astype(jnp.bfloat16)
    root = jnp.where(table[NEED_AT + block] >= ITERS, second, mine)
    total = jnp.zeros(out.shape[1:], jnp.float32)
    for band in range(bands):
        total = total + jnp.dot(root[:, at(band)], cols[band, 0], preferred_element_type=jnp.float32)
    out[0] = total.astype(jnp.bfloat16)


def newton(table, stat, cols):
    bands, shards, home_count, depth, tile = stat.shape
    width = cols.shape[3]
    return pl.pallas_call(
        newton_kernel,
        out_shape=like((home_count, tile, width)),
        grid_spec=pltpu.PrefetchScalarGridSpec(
            num_scalar_prefetch=1,
            grid=(home_count,),
            in_specs=[
                pl.BlockSpec((bands, shards, 1, depth, tile), lambda i, table: (0, 0, i, 0, 0)),
                pl.BlockSpec((bands, 1, tile, width), lambda i, table: (0, i, 0, 0)),
            ],
            out_specs=pl.BlockSpec((1, tile, width), lambda i, table: (i, 0, 0)),
            scratch_shapes=[pltpu.VMEM((bands * tile, bands * tile), jnp.bfloat16)],
        ),
        compiler_params=BIG,
    )(table, stat, cols)


def exchange(array, axis):
    return lax.all_to_all(array, axis, split_axis=0, concat_axis=0, tiled=True)


def shift(array, step):
    return lax.ppermute(array, REP, [(i, (i + step) % BANDS) for i in range(BANDS)])


def after(array, other):
    return lax.optimization_barrier((array, other))[0]


def tables(owner_map, iterations, home_count):
    levels, turns, shards = lax.axis_size("zl"), lax.axis_size("y"), lax.axis_size(BLK)
    my_level, my_turn, my_blk = lax.axis_index("zl"), lax.axis_index("y"), lax.axis_index(BLK)
    my_own = lax.axis_index(OWN)
    total_blocks = owner_map.shape[0]
    column = turns * home_count
    position = jnp.arange(total_blocks, dtype=jnp.int32)
    same = owner_map[:, None] == owner_map[None, :]
    slot = jnp.sum(jnp.where(same & (position[None, :] < position[:, None]), 1, 0), axis=1)
    place_ids = jnp.arange(levels * turns * shards, dtype=jnp.int32)
    lands = (owner_map * shards + slot)[None, :] == place_ids[:, None]
    holder = jnp.sum(jnp.where(lands, position[None, :] + 1, 0), axis=1) - 1
    holder = holder.reshape(levels, turns, shards)
    mine = holder[my_level, my_turn, my_blk]
    from_ring = (owner_map // turns) * shards + slot
    cut = lax.dynamic_slice_in_dim
    return jnp.concatenate(
        [
            jnp.stack([lax.axis_index(REP), my_blk]),
            cut(owner_map, my_own * home_count, home_count) % turns,
            cut(iterations, my_own * home_count, home_count),
            jnp.maximum(holder, 0)[my_level, my_turn] // column,
            jnp.where(mine >= 0, 1, 0)[None],
            cut(from_ring, my_level * column, column),
            (jnp.maximum(holder, 0) % column)[:, my_turn].reshape(-1),
        ]
    ).astype(jnp.int32)


def body(partial_grads, owner_map, iterations, slot_history):
    turns, shards = lax.axis_size("y"), lax.axis_size(BLK)
    ring = lax.axis_size("zl") * shards
    my_blk = lax.axis_index(BLK)
    _, home_count, order_full, width = partial_grads.shape
    tile = order_full // BANDS
    size = tile // shards
    depth = STEPS * size
    history = pltpu.with_memory_space_constraint(slot_history[0, 0], pltpu.HBM)
    table = tables(owner_map, iterations, home_count)
    place = jnp.stack([lax.axis_index(REP), my_blk]).astype(jnp.int32)

    history_ring = exchange(cut_history(place, history, ring, tile, shards), RING)

    partials = call(
        fan_kernel, [place, partial_grads[0]], [like((home_count, tile, width))] * BANDS
    )
    partials = [partials[0]] + [shift(partials[step], step) for step in range(1, BANDS)]
    grad_tile = call(sum_kernel, [place, *partials], like((home_count, tile, width)))
    grad_cols = lax.all_gather(grad_tile, REP, axis=0, tiled=False)

    grad_band = lax.all_gather(grad_tile, BLK, axis=0, tiled=False)

    history_sent = take(table, after(history_ring, grad_band), HISTORY_AT)
    history_sent = history_sent.reshape(turns, home_count, depth, tile)
    history_came = exchange(history_sent, "y")

    mine = lax.dynamic_slice_in_dim(grad_band, my_blk * size, size, 2)
    slices = [shift(mine, -step) for step in range(1, STEPS)]
    gram, gram_sent = call(
        gram_kernel,
        [place, grad_band, *slices],
        [like((home_count, depth, tile), jnp.float32), like((turns, home_count, depth, tile))],
    )
    stat = call(stat_kernel, [table, gram, history_came], like((home_count, depth, tile)))
    stat_band = lax.all_gather(stat, BLK, axis=0, tiled=False)
    gram_came = exchange(gram_sent, "y")
    stat_full = lax.all_gather(after(stat_band, gram_came), REP, axis=0, tiled=False)

    gram_sent = take(table, gram_came.reshape(ring, depth, tile), GRAM_AT)
    gram_level = exchange(gram_sent, "zl")
    gram_slot = call(choose_kernel, [table, gram_level], like((shards, depth, tile)))
    gram_slot = exchange(gram_slot, BLK)
    band, turned = call(
        turn_kernel,
        [table, gram_slot],
        [like((STEPS * tile, tile)), like((BANDS, tile, tile))],
    )
    directions = newton(
        table,
        pltpu.with_memory_space_constraint(stat_full, pltpu.HBM),
        pltpu.with_memory_space_constraint(grad_cols, pltpu.HBM),
    )
    turned = after(exchange(turned, REP), directions)
    new_rows = finish(table, history, band, turned)
    return (directions, new_rows[None, None])


def solution(mesh):
    fine = Mesh(mesh.devices.reshape(4, 2, 4, 8, 4), ("x", "core", "zl", "y", "zh"))
    return jax.shard_map(
        body,
        mesh=fine,
        in_specs=(P(REP, OWN, None, BLK), P(), P(), P(OWN, BLK, None, None)),
        out_specs=(P(OWN, REP, BLK), P(OWN, BLK, REP, None)),
        check_vma=False,
    )
```

```python
import math

import jax
import jax.numpy as jnp
from jax import lax
from jax.experimental import pallas as pl
from jax.experimental.pallas import tpu as pltpu
from jax.sharding import Mesh, PartitionSpec as P

ITERS = 2


DECAY = 0.5
DAMPING = 0.05

REP = ("x", "core")
OWN = ("zl", "y")
BLK = "zh"

BIG = pltpu.CompilerParams(vmem_limit_bytes=40 * 1024 * 1024)
SCALARS = pl.BlockSpec(memory_space=pltpu.SMEM)
WHOLE = pl.BlockSpec(memory_space=pltpu.VMEM)

BANDS, STEPS = 8, 5
REP_AT, BLK_AT, TURN_AT, NEED_AT, LEVEL_AT, HAS_AT, HISTORY_AT, GRAM_AT = 0, 1, 2, 4, 6, 10, 11, 27


def ds(start, size, unit):
    return pl.ds(pl.multiple_of(start, unit), size)


def like(shape, dtype=jnp.bfloat16):
    return jax.ShapeDtypeStruct(shape, dtype)


def call(kernel, ins, outs, in_specs=None, scratch=()):
    many = isinstance(outs, (list, tuple))
    return pl.pallas_call(
        kernel,
        out_shape=outs,
        in_specs=in_specs or [SCALARS] + [WHOLE] * (len(ins) - 1),
        out_specs=[WHOLE] * len(outs) if many else WHOLE,
        scratch_shapes=list(scratch),
        compiler_params=BIG,
    )(*ins)


def split_kernel(table, grads, out):
    rows = out.shape[2]
    for band in range(out.shape[0]):
        out[band] = grads[:, band * rows : (band + 1) * rows]


def sum_kernel(table, parts, out):
    total = parts[0].astype(jnp.float32)
    for band in range(1, parts.shape[0]):
        total = total + parts[band].astype(jnp.float32)
    out[...] = total.astype(jnp.bfloat16)


def history_kernel(table, column, *outs):
    tile = column.shape[1]
    shards = len(outs)
    size = tile // shards
    for turn, out in enumerate(outs):
        part = lax.rem(table[BLK_AT] + turn, shards)
        for step in range(STEPS):
            start = lax.rem(table[REP_AT] + step, BANDS) * tile + part * size
            out[step * size : (step + 1) * size] = column[ds(start, size, size), :]


def cut_history(table, history, tile, shards):
    order_full = history.shape[0]
    shape = (STEPS * tile // shards, tile)
    return pl.pallas_call(
        history_kernel,
        out_shape=[like(shape)] * shards,
        grid_spec=pltpu.PrefetchScalarGridSpec(
            num_scalar_prefetch=1,
            grid=(1,),
            in_specs=[pl.BlockSpec((order_full, tile), lambda i, table: (0, table[REP_AT]))],
            out_specs=[pl.BlockSpec(shape, lambda i, table: (0, 0))] * shards,
        ),
        compiler_params=BIG,
    )(table, history)


def spread_kernel(table, *refs):
    *arrived, out = refs
    shards = len(arrived)
    for turn, ref in enumerate(arrived):
        slot = lax.rem(table[BLK_AT] + shards - turn, shards)
        for level in range(out.shape[0] // shards):
            out[level * shards + slot] = ref[...]


def take(table, tiles, first):
    def kernel(table, tiles, out):
        for place in range(out.shape[0]):
            out[place] = tiles[table[first + place]]

    return call(kernel, [table, tiles], like(tiles.shape))


def gram_kernel(table, band, *refs):
    *slices, out, sent = refs
    shards, home_count, tile, _ = band.shape
    size = tile // shards
    order_full = BANDS * tile
    start = table[BLK_AT] * size
    for block in range(home_count):
        total = jnp.zeros((STEPS * size, tile), jnp.float32)
        for shard in range(shards):
            left = [band[shard, block, ds(start, size, size), :]]
            left += [ref[shard, block] for ref in slices]
            total = total + lax.dot_general(
                jnp.concatenate(left, axis=0),
                band[shard, block],
                (((1,), (1,)), ((), ())),
                preferred_element_type=jnp.float32,
            )
        total = total * ((1.0 - DECAY) / order_full)
        out[block] = total
        for turn in range(sent.shape[0]):
            sent[turn, block] = total.astype(jnp.bfloat16)


def stat_kernel(table, gram, came, out):
    home_count, depth, tile = out.shape
    size = depth // STEPS
    row_ids = lax.broadcasted_iota(jnp.int32, (depth, tile), 0)
    col_ids = lax.broadcasted_iota(jnp.int32, (depth, tile), 1)
    on = (row_ids < size) & (row_ids + table[BLK_AT] * size == col_ids)
    damping = jnp.where(on, DAMPING, 0.0)
    for block in range(home_count):
        history = came[table[TURN_AT + block], block].astype(jnp.float32)
        out[block] = (DECAY * history + gram[block] + damping).astype(jnp.bfloat16)


def choose_kernel(table, came, out):
    shards = out.shape[0]
    for shard in range(shards):
        out[shard] = came[table[LEVEL_AT + shard] * shards + shard]


def turn_kernel(table, came, band, sent):
    tile = sent.shape[1]
    size = came.shape[1] // STEPS
    shards = tile // size
    for shard in range(shards):
        part = came[shard]
        for step in range(STEPS):
            start = step * tile + shard * size
            band[start : start + size] = part[step * size : (step + 1) * size]
    sent[...] = jnp.zeros_like(sent)
    for step in range(1, STEPS):
        sent[lax.rem(table[REP_AT] + step, BANDS)] = band[step * tile : (step + 1) * tile]


def finish_kernel(table, rows, band, came, out):
    tile = rows.shape[0]
    rep = table[REP_AT]

    def put(column, gram, damping=None):
        columns = ds(column * tile, tile, tile)
        history = rows[:, columns].astype(jnp.float32)
        fresh = DECAY * history + gram
        if damping is not None:
            fresh = fresh + damping
        out[:, columns] = jnp.where(table[HAS_AT] > 0, fresh, history).astype(jnp.bfloat16)

    row_ids = lax.broadcasted_iota(jnp.int32, (tile, tile), 0)
    col_ids = lax.broadcasted_iota(jnp.int32, (tile, tile), 1)
    put(rep, band[:tile].astype(jnp.float32), jnp.where(row_ids == col_ids, DAMPING, 0.0))
    for step in range(1, STEPS):
        other = lax.rem(rep + BANDS - step, BANDS)
        put(other, came[other].astype(jnp.float32))
        if step < STEPS - 1:
            mine = band[step * tile : (step + 1) * tile].astype(jnp.float32)
            put(lax.rem(rep + step, BANDS), mine.T)


def finish(table, history, band, came):
    tile, order_full = band.shape[1], history.shape[1]
    return pl.pallas_call(
        finish_kernel,
        out_shape=like((tile, order_full)),
        grid_spec=pltpu.PrefetchScalarGridSpec(
            num_scalar_prefetch=1,
            grid=(1,),
            in_specs=[
                pl.BlockSpec((tile, order_full), lambda i, table: (table[REP_AT], 0)),
                pl.BlockSpec(band.shape, lambda i, table: (0, 0)),
                pl.BlockSpec(came.shape, lambda i, table: (0, 0, 0)),
            ],
            out_specs=pl.BlockSpec((tile, order_full), lambda i, table: (0, 0)),
        ),
        compiler_params=BIG,
    )(table, history, band, came)


def newton_kernel(table, stat, cols, out, full):
    bands, shards, _, depth, tile = stat.shape
    size = depth // STEPS
    order_full = bands * tile
    block = pl.program_id(0)
    squares = jnp.zeros((8, tile), jnp.float32)
    for band in range(bands):
        for shard in range(shards):
            part = stat[band, shard, 0].astype(jnp.float32)
            part = (part * part).reshape(-1, 8, tile)
            ends, middle = size // 8, (STEPS - 1) * size // 8
            squares = squares + jnp.sum(part, axis=0) + jnp.sum(part[ends:middle], axis=0)
    frobenius = jnp.sqrt(jnp.sum(squares, keepdims=True)[:1, :1])
    norm_scale = math.sqrt(order_full) / (2.0 * frobenius)

    def at(index):
        return slice(index * tile, (index + 1) * tile)

    for band in range(bands):
        for shard in range(shards):
            part = (stat[band, shard, 0].astype(jnp.float32) * norm_scale).astype(jnp.bfloat16)
            for step in range(STEPS):
                start = (band + step) % bands * tile + shard * size
                full[start : start + size, at(band)] = part[step * size : (step + 1) * size]
    for band in range(bands):
        for step in range(1, STEPS - 1):
            other = (band + step) % bands
            full[at(band), at(other)] = full[at(other), at(band)].T

    row_ids = lax.broadcasted_iota(jnp.int32, (tile, tile), 0)
    col_ids = lax.broadcasted_iota(jnp.int32, (tile, tile), 1)
    diagonals = []
    for band in range(bands):
        corner = full[at(band), at(band)].astype(jnp.float32)
        values = jnp.sum(jnp.where(row_ids == col_ids, corner, 0.0), axis=0, keepdims=True)
        rounded = (1.5 - 0.5 * values).astype(jnp.bfloat16).astype(jnp.float32)
        diagonals.append(rounded + 0.5 * values)
    diagonal = jnp.concatenate(diagonals, axis=1)

    def times_scaled(left):
        return jnp.dot(left, full[...], preferred_element_type=jnp.float32)

    def times_factor(left):
        return left.astype(jnp.float32) * diagonal - 0.5 * times_scaled(left)

    first = table[REP_AT] * tile
    wide_rows = lax.broadcasted_iota(jnp.int32, (tile, order_full), 0) + first
    wide_cols = lax.broadcasted_iota(jnp.int32, (tile, order_full), 1)
    identity = jnp.where(wide_rows == wide_cols, 1.5, 0.0)
    mine = full[ds(first, tile, tile), :].astype(jnp.float32)
    mine = (identity - 0.5 * mine).astype(jnp.bfloat16)
    product = times_factor(times_scaled(mine).astype(jnp.bfloat16))
    update = (identity - 0.5 * product).astype(jnp.bfloat16)
    second = times_factor(update).astype(jnp.bfloat16)
    root = jnp.where(table[NEED_AT + block] >= ITERS, second, mine)
    total = jnp.zeros(out.shape[1:], jnp.float32)
    for band in range(bands):
        total = total + jnp.dot(root[:, at(band)], cols[band, 0], preferred_element_type=jnp.float32)
    out[0] = total.astype(jnp.bfloat16)


def newton(table, stat, cols):
    bands, shards, home_count, depth, tile = stat.shape
    width = cols.shape[3]
    return pl.pallas_call(
        newton_kernel,
        out_shape=like((home_count, tile, width)),
        grid_spec=pltpu.PrefetchScalarGridSpec(
            num_scalar_prefetch=1,
            grid=(home_count,),
            in_specs=[
                pl.BlockSpec((bands, shards, 1, depth, tile), lambda i, table: (0, 0, i, 0, 0)),
                pl.BlockSpec((bands, 1, tile, width), lambda i, table: (0, i, 0, 0)),
            ],
            out_specs=pl.BlockSpec((1, tile, width), lambda i, table: (i, 0, 0)),
            scratch_shapes=[pltpu.VMEM((bands * tile, bands * tile), jnp.bfloat16)],
        ),
        compiler_params=BIG,
    )(table, stat, cols)


def exchange(array, axis):
    return lax.all_to_all(array, axis, split_axis=0, concat_axis=0, tiled=True)


def shift(array, step):
    return lax.ppermute(array, REP, [(i, (i + step) % BANDS) for i in range(BANDS)])


def swap(parts, count):
    return [parts[0]] + [
        lax.ppermute(parts[turn], BLK, [(i, (i + turn) % count) for i in range(count)])
        for turn in range(1, count)
    ]


def after(array, other):
    return lax.optimization_barrier((array, other))[0]


def tables(owner_map, iterations, home_count):
    levels, turns, shards = lax.axis_size("zl"), lax.axis_size("y"), lax.axis_size(BLK)
    my_level, my_turn, my_blk = lax.axis_index("zl"), lax.axis_index("y"), lax.axis_index(BLK)
    my_own = lax.axis_index(OWN)
    total_blocks = owner_map.shape[0]
    column = turns * home_count
    position = jnp.arange(total_blocks, dtype=jnp.int32)
    same = owner_map[:, None] == owner_map[None, :]
    slot = jnp.sum(jnp.where(same & (position[None, :] < position[:, None]), 1, 0), axis=1)
    place_ids = jnp.arange(levels * turns * shards, dtype=jnp.int32)
    lands = (owner_map * shards + slot)[None, :] == place_ids[:, None]
    holder = jnp.sum(jnp.where(lands, position[None, :] + 1, 0), axis=1) - 1
    holder = holder.reshape(levels, turns, shards)
    mine = holder[my_level, my_turn, my_blk]
    from_ring = (owner_map // turns) * shards + slot
    cut = lax.dynamic_slice_in_dim
    return jnp.concatenate(
        [
            jnp.stack([lax.axis_index(REP), my_blk]),
            cut(owner_map, my_own * home_count, home_count) % turns,
            cut(iterations, my_own * home_count, home_count),
            jnp.maximum(holder, 0)[my_level, my_turn] // column,
            jnp.where(mine >= 0, 1, 0)[None],
            cut(from_ring, my_level * column, column),
            (jnp.maximum(holder, 0) % column)[:, my_turn].reshape(-1),
        ]
    ).astype(jnp.int32)


def body(partial_grads, owner_map, iterations, slot_history):
    turns, shards = lax.axis_size("y"), lax.axis_size(BLK)
    ring = lax.axis_size("zl") * shards
    my_blk = lax.axis_index(BLK)
    _, home_count, order_full, width = partial_grads.shape
    tile = order_full // BANDS
    size = tile // shards
    depth = STEPS * size
    history = pltpu.with_memory_space_constraint(slot_history[0, 0], pltpu.HBM)
    table = tables(owner_map, iterations, home_count)
    place = jnp.stack([lax.axis_index(REP), my_blk]).astype(jnp.int32)

    outgoing = call(split_kernel, [place, partial_grads[0]], like((BANDS, home_count, tile, width)))
    history_parts = swap(cut_history(place, history, tile, shards), shards)
    partials = exchange(outgoing, REP)
    grad_tile = call(sum_kernel, [place, partials], like((home_count, tile, width)))

    history_sent = call(spread_kernel, [place, *history_parts], like((ring, depth, tile)))
    history_level = exchange(after(history_sent, grad_tile), "zl")
    grad_cols = lax.all_gather(grad_tile, REP, axis=0, tiled=False)

    grad_band = lax.all_gather(grad_tile, BLK, axis=0, tiled=False)

    history_sent = take(table, after(history_level, grad_band), HISTORY_AT)
    history_sent = history_sent.reshape(turns, home_count, depth, tile)
    history_came = exchange(history_sent, "y")

    mine = lax.dynamic_slice_in_dim(grad_band, my_blk * size, size, 2)
    slices = [shift(mine, -step) for step in range(1, STEPS)]
    gram, gram_sent = call(
        gram_kernel,
        [place, grad_band, *slices],
        [like((home_count, depth, tile), jnp.float32), like((turns, home_count, depth, tile))],
    )
    stat = call(stat_kernel, [table, gram, history_came], like((home_count, depth, tile)))
    stat_band = lax.all_gather(stat, BLK, axis=0, tiled=False)
    gram_came = exchange(gram_sent, "y")
    stat_full = lax.all_gather(after(stat_band, gram_came), REP, axis=0, tiled=False)

    gram_sent = take(table, gram_came.reshape(ring, depth, tile), GRAM_AT)
    gram_level = exchange(gram_sent, "zl")
    gram_slot = call(choose_kernel, [table, gram_level], like((shards, depth, tile)))
    gram_slot = exchange(gram_slot, BLK)
    band, turned = call(
        turn_kernel,
        [table, gram_slot],
        [like((STEPS * tile, tile)), like((BANDS, tile, tile))],
    )
    directions = newton(
        table,
        pltpu.with_memory_space_constraint(stat_full, pltpu.HBM),
        pltpu.with_memory_space_constraint(grad_cols, pltpu.HBM),
    )
    turned = after(exchange(turned, REP), directions)
    new_rows = finish(table, history, band, turned)
    return (directions, new_rows[None, None])


def solution(mesh):
    fine = Mesh(mesh.devices.reshape(4, 2, 4, 8, 4), ("x", "core", "zl", "y", "zh"))
    return jax.shard_map(
        body,
        mesh=fine,
        in_specs=(P(REP, OWN, None, BLK), P(), P(), P(OWN, BLK, None, None)),
        out_specs=(P(OWN, REP, BLK), P(OWN, BLK, REP, None)),
        check_vma=False,
    )
```

```python
import math

import jax
import jax.numpy as jnp
from jax import lax
from jax.experimental import pallas as pl
from jax.experimental.pallas import tpu as pltpu
from jax.sharding import Mesh, PartitionSpec as P

ITERS = 2


DECAY = 0.5
DAMPING = 0.05

REP = ("x", "core")
OWN = ("zl", "y")
BLK = "zh"
RING = ("zl", "zh")

BIG = pltpu.CompilerParams(vmem_limit_bytes=40 * 1024 * 1024)
SCALARS = pl.BlockSpec(memory_space=pltpu.SMEM)
WHOLE = pl.BlockSpec(memory_space=pltpu.VMEM)

BANDS, STEPS = 8, 5
REP_AT, BLK_AT, TURN_AT, NEED_AT, LEVEL_AT, HAS_AT, HISTORY_AT, GRAM_AT = 0, 1, 2, 4, 6, 10, 11, 27


def ds(start, size, unit):
    return pl.ds(pl.multiple_of(start, unit), size)


def like(shape, dtype=jnp.bfloat16):
    return jax.ShapeDtypeStruct(shape, dtype)


def call(kernel, ins, outs, in_specs=None, scratch=()):
    many = isinstance(outs, (list, tuple))
    return pl.pallas_call(
        kernel,
        out_shape=outs,
        in_specs=in_specs or [SCALARS] + [WHOLE] * (len(ins) - 1),
        out_specs=[WHOLE] * len(outs) if many else WHOLE,
        scratch_shapes=list(scratch),
        compiler_params=BIG,
    )(*ins)


def fan_kernel(table, grads, kept, sent):
    pairs, _, rows, _ = kept.shape
    pair, core = lax.div(table[REP_AT], 2), lax.rem(table[REP_AT], 2)
    for step in range(pairs):
        first = lax.rem(pair + step, pairs) * 2
        kept[step] = grads[:, ds((first + core) * rows, rows, rows), :]
        sent[step] = grads[:, ds((first + 1 - core) * rows, rows, rows), :]


def pair_kernel(table, kept, came, *outs):
    for step, out in enumerate(outs):
        total = kept[step].astype(jnp.float32) + came[step].astype(jnp.float32)
        out[...] = total.astype(jnp.bfloat16)


def sum_kernel(table, *refs):
    *ins, out = refs
    total = ins[0][...].astype(jnp.float32)
    for ref in ins[1:]:
        total = total + ref[...].astype(jnp.float32)
    out[...] = total.astype(jnp.bfloat16)


def history_kernel(table, column, out):
    tile = column.shape[1]
    shards = 4
    size = tile // shards
    for step in range(STEPS):
        start = lax.rem(table[REP_AT] + step, BANDS) * tile
        for shard in range(shards):
            piece = column[ds(start + shard * size, size, size), :]
            for level in range(out.shape[0] // shards):
                out[level * shards + shard, step * size : (step + 1) * size] = piece


def cut_history(table, history, places, tile, shards):
    order_full = history.shape[0]
    shape = (places, STEPS * tile // shards, tile)
    return pl.pallas_call(
        history_kernel,
        out_shape=like(shape),
        grid_spec=pltpu.PrefetchScalarGridSpec(
            num_scalar_prefetch=1,
            grid=(1,),
            in_specs=[pl.BlockSpec((order_full, tile), lambda i, table: (0, table[REP_AT]))],
            out_specs=pl.BlockSpec(shape, lambda i, table: (0, 0, 0)),
        ),
        compiler_params=BIG,
    )(table, history)


def take(table, tiles, first):
    def kernel(table, tiles, out):
        for place in range(out.shape[0]):
            out[place] = tiles[table[first + place]]

    return call(kernel, [table, tiles], like(tiles.shape))


def gram_kernel(table, band, *refs):
    *slices, out, sent = refs
    shards, home_count, tile, _ = band.shape
    size = tile // shards
    order_full = BANDS * tile
    start = table[BLK_AT] * size
    for block in range(home_count):
        total = jnp.zeros((STEPS * size, tile), jnp.float32)
        for shard in range(shards):
            left = [band[shard, block, ds(start, size, size), :]]
            left += [ref[shard, block] for ref in slices]
            total = total + lax.dot_general(
                jnp.concatenate(left, axis=0),
                band[shard, block],
                (((1,), (1,)), ((), ())),
                preferred_element_type=jnp.float32,
            )
        total = total * ((1.0 - DECAY) / order_full)
        out[block] = total
        for turn in range(sent.shape[0]):
            sent[turn, block] = total.astype(jnp.bfloat16)


def stat_kernel(table, gram, came, out):
    home_count, depth, tile = out.shape
    size = depth // STEPS
    row_ids = lax.broadcasted_iota(jnp.int32, (depth, tile), 0)
    col_ids = lax.broadcasted_iota(jnp.int32, (depth, tile), 1)
    on = (row_ids < size) & (row_ids + table[BLK_AT] * size == col_ids)
    damping = jnp.where(on, DAMPING, 0.0)
    for block in range(home_count):
        history = came[table[TURN_AT + block], block].astype(jnp.float32)
        out[block] = (DECAY * history + gram[block] + damping).astype(jnp.bfloat16)


def choose_kernel(table, came, out):
    shards = out.shape[0]
    for shard in range(shards):
        out[shard] = came[table[LEVEL_AT + shard] * shards + shard]


def turn_kernel(table, came, band, sent):
    tile = sent.shape[1]
    size = came.shape[1] // STEPS
    shards = tile // size
    for shard in range(shards):
        part = came[shard]
        for step in range(STEPS):
            start = step * tile + shard * size
            band[start : start + size] = part[step * size : (step + 1) * size]
    sent[...] = jnp.zeros_like(sent)
    for step in range(1, STEPS):
        sent[lax.rem(table[REP_AT] + step, BANDS)] = band[step * tile : (step + 1) * tile]


def finish_kernel(table, rows, band, came, out):
    tile = rows.shape[0]
    rep = table[REP_AT]

    def put(column, gram, damping=None):
        columns = ds(column * tile, tile, tile)
        history = rows[:, columns].astype(jnp.float32)
        fresh = DECAY * history + gram
        if damping is not None:
            fresh = fresh + damping
        out[:, columns] = jnp.where(table[HAS_AT] > 0, fresh, history).astype(jnp.bfloat16)

    row_ids = lax.broadcasted_iota(jnp.int32, (tile, tile), 0)
    col_ids = lax.broadcasted_iota(jnp.int32, (tile, tile), 1)
    put(rep, band[:tile].astype(jnp.float32), jnp.where(row_ids == col_ids, DAMPING, 0.0))
    for step in range(1, STEPS):
        other = lax.rem(rep + BANDS - step, BANDS)
        put(other, came[other].astype(jnp.float32))
        if step < STEPS - 1:
            mine = band[step * tile : (step + 1) * tile].astype(jnp.float32)
            put(lax.rem(rep + step, BANDS), mine.T)


def finish(table, history, band, came):
    tile, order_full = band.shape[1], history.shape[1]
    return pl.pallas_call(
        finish_kernel,
        out_shape=like((tile, order_full)),
        grid_spec=pltpu.PrefetchScalarGridSpec(
            num_scalar_prefetch=1,
            grid=(1,),
            in_specs=[
                pl.BlockSpec((tile, order_full), lambda i, table: (table[REP_AT], 0)),
                pl.BlockSpec(band.shape, lambda i, table: (0, 0)),
                pl.BlockSpec(came.shape, lambda i, table: (0, 0, 0)),
            ],
            out_specs=pl.BlockSpec((tile, order_full), lambda i, table: (0, 0)),
        ),
        compiler_params=BIG,
    )(table, history, band, came)


def newton_kernel(table, stat, cols, out, full):
    bands, shards, _, depth, tile = stat.shape
    size = depth // STEPS
    order_full = bands * tile
    block = pl.program_id(0)
    squares = jnp.zeros((8, tile), jnp.float32)
    for band in range(bands):
        for shard in range(shards):
            part = stat[band, shard, 0].astype(jnp.float32)
            part = (part * part).reshape(-1, 8, tile)
            ends, middle = size // 8, (STEPS - 1) * size // 8
            squares = squares + jnp.sum(part, axis=0) + jnp.sum(part[ends:middle], axis=0)
    frobenius = jnp.sqrt(jnp.sum(squares, keepdims=True)[:1, :1])
    norm_scale = math.sqrt(order_full) / (2.0 * frobenius)

    def at(index):
        return slice(index * tile, (index + 1) * tile)

    for band in range(bands):
        for shard in range(shards):
            part = (stat[band, shard, 0].astype(jnp.float32) * norm_scale).astype(jnp.bfloat16)
            for step in range(STEPS):
                start = (band + step) % bands * tile + shard * size
                full[start : start + size, at(band)] = part[step * size : (step + 1) * size]
    for band in range(bands):
        for step in range(1, STEPS - 1):
            other = (band + step) % bands
            full[at(band), at(other)] = full[at(other), at(band)].T

    row_ids = lax.broadcasted_iota(jnp.int32, (tile, tile), 0)
    col_ids = lax.broadcasted_iota(jnp.int32, (tile, tile), 1)
    diagonals = []
    for band in range(bands):
        corner = full[at(band), at(band)].astype(jnp.float32)
        values = jnp.sum(jnp.where(row_ids == col_ids, corner, 0.0), axis=0, keepdims=True)
        rounded = (1.5 - 0.5 * values).astype(jnp.bfloat16).astype(jnp.float32)
        diagonals.append(rounded + 0.5 * values)
    diagonal = jnp.concatenate(diagonals, axis=1)

    def times_scaled(left):
        return jnp.dot(left, full[...], preferred_element_type=jnp.float32)

    def times_factor(left):
        return left.astype(jnp.float32) * diagonal - 0.5 * times_scaled(left)

    first = table[REP_AT] * tile
    wide_rows = lax.broadcasted_iota(jnp.int32, (tile, order_full), 0) + first
    wide_cols = lax.broadcasted_iota(jnp.int32, (tile, order_full), 1)
    identity = jnp.where(wide_rows == wide_cols, 1.5, 0.0)
    mine = full[ds(first, tile, tile), :].astype(jnp.float32)
    mine = (identity - 0.5 * mine).astype(jnp.bfloat16)
    product = times_factor(times_scaled(mine).astype(jnp.bfloat16))
    update = (identity - 0.5 * product).astype(jnp.bfloat16)
    second = times_factor(update).astype(jnp.bfloat16)
    root = jnp.where(table[NEED_AT + block] >= ITERS, second, mine)
    total = jnp.zeros(out.shape[1:], jnp.float32)
    for band in range(bands):
        total = total + jnp.dot(root[:, at(band)], cols[band, 0], preferred_element_type=jnp.float32)
    out[0] = total.astype(jnp.bfloat16)


def newton(table, stat, cols):
    bands, shards, home_count, depth, tile = stat.shape
    width = cols.shape[3]
    return pl.pallas_call(
        newton_kernel,
        out_shape=like((home_count, tile, width)),
        grid_spec=pltpu.PrefetchScalarGridSpec(
            num_scalar_prefetch=1,
            grid=(home_count,),
            in_specs=[
                pl.BlockSpec((bands, shards, 1, depth, tile), lambda i, table: (0, 0, i, 0, 0)),
                pl.BlockSpec((bands, 1, tile, width), lambda i, table: (0, i, 0, 0)),
            ],
            out_specs=pl.BlockSpec((1, tile, width), lambda i, table: (i, 0, 0)),
            scratch_shapes=[pltpu.VMEM((bands * tile, bands * tile), jnp.bfloat16)],
        ),
        compiler_params=BIG,
    )(table, stat, cols)


def exchange(array, axis):
    return lax.all_to_all(array, axis, split_axis=0, concat_axis=0, tiled=True)


def shift(array, step):
    return lax.ppermute(array, REP, [(i, (i + step) % BANDS) for i in range(BANDS)])


def after(array, other):
    return lax.optimization_barrier((array, other))[0]


def tables(owner_map, iterations, home_count):
    levels, turns, shards = lax.axis_size("zl"), lax.axis_size("y"), lax.axis_size(BLK)
    my_level, my_turn, my_blk = lax.axis_index("zl"), lax.axis_index("y"), lax.axis_index(BLK)
    my_own = lax.axis_index(OWN)
    total_blocks = owner_map.shape[0]
    column = turns * home_count
    position = jnp.arange(total_blocks, dtype=jnp.int32)
    same = owner_map[:, None] == owner_map[None, :]
    slot = jnp.sum(jnp.where(same & (position[None, :] < position[:, None]), 1, 0), axis=1)
    place_ids = jnp.arange(levels * turns * shards, dtype=jnp.int32)
    lands = (owner_map * shards + slot)[None, :] == place_ids[:, None]
    holder = jnp.sum(jnp.where(lands, position[None, :] + 1, 0), axis=1) - 1
    holder = holder.reshape(levels, turns, shards)
    mine = holder[my_level, my_turn, my_blk]
    from_ring = (owner_map // turns) * shards + slot
    cut = lax.dynamic_slice_in_dim
    return jnp.concatenate(
        [
            jnp.stack([lax.axis_index(REP), my_blk]),
            cut(owner_map, my_own * home_count, home_count) % turns,
            cut(iterations, my_own * home_count, home_count),
            jnp.maximum(holder, 0)[my_level, my_turn] // column,
            jnp.where(mine >= 0, 1, 0)[None],
            cut(from_ring, my_level * column, column),
            (jnp.maximum(holder, 0) % column)[:, my_turn].reshape(-1),
        ]
    ).astype(jnp.int32)


def body(partial_grads, owner_map, iterations, slot_history):
    turns, shards = lax.axis_size("y"), lax.axis_size(BLK)
    ring = lax.axis_size("zl") * shards
    my_blk = lax.axis_index(BLK)
    _, home_count, order_full, width = partial_grads.shape
    tile = order_full // BANDS
    size = tile // shards
    depth = STEPS * size
    history = pltpu.with_memory_space_constraint(slot_history[0, 0], pltpu.HBM)
    table = tables(owner_map, iterations, home_count)
    place = jnp.stack([lax.axis_index(REP), my_blk]).astype(jnp.int32)

    pairs = lax.axis_size("x")
    half = like((pairs, home_count, tile, width))
    kept, sent = call(fan_kernel, [place, partial_grads[0]], [half, half])
    came = lax.ppermute(sent, "core", [(0, 1), (1, 0)])

    history_ring = exchange(cut_history(after(place, sent), history, ring, tile, shards), RING)

    chip = call(pair_kernel, [place, kept, came], [like((home_count, tile, width))] * pairs)
    partials = [chip[0]] + [
        lax.ppermute(chip[step], "x", [(i, (i + step) % pairs) for i in range(pairs)])
        for step in range(1, pairs)
    ]
    grad_tile = call(sum_kernel, [place, *partials], like((home_count, tile, width)))
    grad_cols = lax.all_gather(grad_tile, REP, axis=0, tiled=False)

    grad_band = lax.all_gather(grad_tile, BLK, axis=0, tiled=False)

    history_sent = take(table, after(history_ring, grad_band), HISTORY_AT)
    history_sent = history_sent.reshape(turns, home_count, depth, tile)
    history_came = exchange(history_sent, "y")

    mine = lax.dynamic_slice_in_dim(grad_band, my_blk * size, size, 2)
    slices = [shift(mine, -step) for step in range(1, STEPS)]
    gram, gram_sent = call(
        gram_kernel,
        [place, grad_band, *slices],
        [like((home_count, depth, tile), jnp.float32), like((turns, home_count, depth, tile))],
    )
    stat = call(stat_kernel, [table, gram, history_came], like((home_count, depth, tile)))
    stat_band = lax.all_gather(stat, BLK, axis=0, tiled=False)
    gram_came = exchange(gram_sent, "y")
    stat_full = lax.all_gather(after(stat_band, gram_came), REP, axis=0, tiled=False)

    gram_sent = take(table, gram_came.reshape(ring, depth, tile), GRAM_AT)
    gram_level = exchange(gram_sent, "zl")
    gram_slot = call(choose_kernel, [table, gram_level], like((shards, depth, tile)))
    gram_slot = exchange(gram_slot, BLK)
    band, turned = call(
        turn_kernel,
        [table, gram_slot],
        [like((STEPS * tile, tile)), like((BANDS, tile, tile))],
    )
    directions = newton(
        table,
        pltpu.with_memory_space_constraint(stat_full, pltpu.HBM),
        pltpu.with_memory_space_constraint(grad_cols, pltpu.HBM),
    )
    turned = after(exchange(turned, REP), directions)
    new_rows = finish(table, history, band, turned)
    return (directions, new_rows[None, None])


def solution(mesh):
    fine = Mesh(mesh.devices.reshape(4, 2, 4, 8, 4), ("x", "core", "zl", "y", "zh"))
    return jax.shard_map(
        body,
        mesh=fine,
        in_specs=(P(REP, OWN, None, BLK), P(), P(), P(OWN, BLK, None, None)),
        out_specs=(P(OWN, REP, BLK), P(OWN, BLK, REP, None)),
        check_vma=False,
    )
```

```python
import math

import jax
import jax.numpy as jnp
from jax import lax
from jax.experimental import pallas as pl
from jax.experimental.pallas import tpu as pltpu
from jax.sharding import Mesh, PartitionSpec as P

ITERS = 2


DECAY = 0.5
DAMPING = 0.05

REP = ("x", "core")
OWN = ("zl", "y")
BLK = "zh"

BIG = pltpu.CompilerParams(vmem_limit_bytes=40 * 1024 * 1024)
SCALARS = pl.BlockSpec(memory_space=pltpu.SMEM)
WHOLE = pl.BlockSpec(memory_space=pltpu.VMEM)

BANDS, STEPS = 8, 5
REP_AT, BLK_AT, TURN_AT, NEED_AT, LEVEL_AT, HAS_AT, HISTORY_AT, GRAM_AT = 0, 1, 2, 4, 6, 10, 11, 27


def ds(start, size, unit):
    return pl.ds(pl.multiple_of(start, unit), size)


def like(shape, dtype=jnp.bfloat16):
    return jax.ShapeDtypeStruct(shape, dtype)


def call(kernel, ins, outs, in_specs=None, scratch=()):
    many = isinstance(outs, (list, tuple))
    return pl.pallas_call(
        kernel,
        out_shape=outs,
        in_specs=in_specs or [SCALARS] + [WHOLE] * (len(ins) - 1),
        out_specs=[WHOLE] * len(outs) if many else WHOLE,
        scratch_shapes=list(scratch),
        compiler_params=BIG,
    )(*ins)


def fan_kernel(table, grads, kept, sent):
    pairs, _, rows, _ = kept.shape
    pair, core = lax.div(table[REP_AT], 2), lax.rem(table[REP_AT], 2)
    for step in range(pairs):
        first = lax.rem(pair + step, pairs) * 2
        kept[step] = grads[:, ds((first + core) * rows, rows, rows), :]
        sent[step] = grads[:, ds((first + 1 - core) * rows, rows, rows), :]


def pair_kernel(table, kept, came, *outs):
    for step, out in enumerate(outs):
        total = kept[step].astype(jnp.float32) + came[step].astype(jnp.float32)
        out[...] = total.astype(jnp.bfloat16)


def sum_kernel(table, *refs):
    *ins, out = refs
    total = ins[0][...].astype(jnp.float32)
    for ref in ins[1:]:
        total = total + ref[...].astype(jnp.float32)
    out[...] = total.astype(jnp.bfloat16)


def history_kernel(table, column, out):
    shards, _, tile = out.shape
    size = tile // shards
    for step in range(STEPS):
        start = lax.rem(table[REP_AT] + step, BANDS) * tile
        for shard in range(shards):
            piece = column[ds(start + shard * size, size, size), :]
            out[shard, step * size : (step + 1) * size] = piece


def cut_history(table, history, tile, shards):
    order_full = history.shape[0]
    shape = (shards, STEPS * tile // shards, tile)
    return pl.pallas_call(
        history_kernel,
        out_shape=like(shape),
        grid_spec=pltpu.PrefetchScalarGridSpec(
            num_scalar_prefetch=1,
            grid=(1,),
            in_specs=[pl.BlockSpec((order_full, tile), lambda i, table: (0, table[REP_AT]))],
            out_specs=pl.BlockSpec(shape, lambda i, table: (0, 0, 0)),
        ),
        compiler_params=BIG,
    )(table, history)


def take(table, tiles, first):
    def kernel(table, tiles, out):
        for place in range(out.shape[0]):
            out[place] = tiles[table[first + place]]

    return call(kernel, [table, tiles], like(tiles.shape))


def gram_kernel(table, band, *refs):
    *slices, out, sent = refs
    shards, home_count, tile, _ = band.shape
    size = tile // shards
    order_full = BANDS * tile
    start = table[BLK_AT] * size
    for block in range(home_count):
        total = jnp.zeros((STEPS * size, tile), jnp.float32)
        for shard in range(shards):
            left = [band[shard, block, ds(start, size, size), :]]
            left += [ref[shard, block] for ref in slices]
            total = total + lax.dot_general(
                jnp.concatenate(left, axis=0),
                band[shard, block],
                (((1,), (1,)), ((), ())),
                preferred_element_type=jnp.float32,
            )
        total = total * ((1.0 - DECAY) / order_full)
        out[block] = total
        for turn in range(sent.shape[0]):
            sent[turn, block] = total.astype(jnp.bfloat16)


def stat_kernel(table, gram, came, out):
    home_count, depth, tile = out.shape
    size = depth // STEPS
    row_ids = lax.broadcasted_iota(jnp.int32, (depth, tile), 0)
    col_ids = lax.broadcasted_iota(jnp.int32, (depth, tile), 1)
    on = (row_ids < size) & (row_ids + table[BLK_AT] * size == col_ids)
    damping = jnp.where(on, DAMPING, 0.0)
    for block in range(home_count):
        history = came[table[TURN_AT + block], block].astype(jnp.float32)
        out[block] = (DECAY * history + gram[block] + damping).astype(jnp.bfloat16)


def choose_kernel(table, came, out):
    shards = out.shape[0]
    for shard in range(shards):
        out[shard] = came[table[LEVEL_AT + shard] * shards + shard]


def turn_kernel(table, came, band, sent):
    tile = sent.shape[1]
    size = came.shape[1] // STEPS
    shards = tile // size
    for shard in range(shards):
        part = came[shard]
        for step in range(STEPS):
            start = step * tile + shard * size
            band[start : start + size] = part[step * size : (step + 1) * size]
    sent[...] = jnp.zeros_like(sent)
    for step in range(1, STEPS):
        sent[lax.rem(table[REP_AT] + step, BANDS)] = band[step * tile : (step + 1) * tile]


def finish_kernel(table, rows, band, came, out):
    tile = rows.shape[0]
    rep = table[REP_AT]

    def put(column, gram, damping=None):
        columns = ds(column * tile, tile, tile)
        history = rows[:, columns].astype(jnp.float32)
        fresh = DECAY * history + gram
        if damping is not None:
            fresh = fresh + damping
        out[:, columns] = jnp.where(table[HAS_AT] > 0, fresh, history).astype(jnp.bfloat16)

    row_ids = lax.broadcasted_iota(jnp.int32, (tile, tile), 0)
    col_ids = lax.broadcasted_iota(jnp.int32, (tile, tile), 1)
    put(rep, band[:tile].astype(jnp.float32), jnp.where(row_ids == col_ids, DAMPING, 0.0))
    for step in range(1, STEPS):
        other = lax.rem(rep + BANDS - step, BANDS)
        put(other, came[other].astype(jnp.float32))
        if step < STEPS - 1:
            mine = band[step * tile : (step + 1) * tile].astype(jnp.float32)
            put(lax.rem(rep + step, BANDS), mine.T)


def finish(table, history, band, came):
    tile, order_full = band.shape[1], history.shape[1]
    return pl.pallas_call(
        finish_kernel,
        out_shape=like((tile, order_full)),
        grid_spec=pltpu.PrefetchScalarGridSpec(
            num_scalar_prefetch=1,
            grid=(1,),
            in_specs=[
                pl.BlockSpec((tile, order_full), lambda i, table: (table[REP_AT], 0)),
                pl.BlockSpec(band.shape, lambda i, table: (0, 0)),
                pl.BlockSpec(came.shape, lambda i, table: (0, 0, 0)),
            ],
            out_specs=pl.BlockSpec((tile, order_full), lambda i, table: (0, 0)),
        ),
        compiler_params=BIG,
    )(table, history, band, came)


def newton_kernel(table, stat, cols, out, full):
    bands, shards, _, depth, tile = stat.shape
    size = depth // STEPS
    order_full = bands * tile
    block = pl.program_id(0)
    squares = jnp.zeros((8, tile), jnp.float32)
    for band in range(bands):
        for shard in range(shards):
            part = stat[band, shard, 0].astype(jnp.float32)
            part = (part * part).reshape(-1, 8, tile)
            ends, middle = size // 8, (STEPS - 1) * size // 8
            squares = squares + jnp.sum(part, axis=0) + jnp.sum(part[ends:middle], axis=0)
    frobenius = jnp.sqrt(jnp.sum(squares, keepdims=True)[:1, :1])
    norm_scale = math.sqrt(order_full) / (2.0 * frobenius)

    def at(index):
        return slice(index * tile, (index + 1) * tile)

    for band in range(bands):
        for shard in range(shards):
            part = (stat[band, shard, 0].astype(jnp.float32) * norm_scale).astype(jnp.bfloat16)
            for step in range(STEPS):
                start = (band + step) % bands * tile + shard * size
                full[start : start + size, at(band)] = part[step * size : (step + 1) * size]
    for band in range(bands):
        for step in range(1, STEPS - 1):
            other = (band + step) % bands
            full[at(band), at(other)] = full[at(other), at(band)].T

    row_ids = lax.broadcasted_iota(jnp.int32, (tile, tile), 0)
    col_ids = lax.broadcasted_iota(jnp.int32, (tile, tile), 1)
    diagonals = []
    for band in range(bands):
        corner = full[at(band), at(band)].astype(jnp.float32)
        values = jnp.sum(jnp.where(row_ids == col_ids, corner, 0.0), axis=0, keepdims=True)
        rounded = (1.5 - 0.5 * values).astype(jnp.bfloat16).astype(jnp.float32)
        diagonals.append(rounded + 0.5 * values)
    diagonal = jnp.concatenate(diagonals, axis=1)

    def times_scaled(left):
        return jnp.dot(left, full[...], preferred_element_type=jnp.float32)

    def times_factor(left):
        return left.astype(jnp.float32) * diagonal - 0.5 * times_scaled(left)

    first = table[REP_AT] * tile
    wide_rows = lax.broadcasted_iota(jnp.int32, (tile, order_full), 0) + first
    wide_cols = lax.broadcasted_iota(jnp.int32, (tile, order_full), 1)
    identity = jnp.where(wide_rows == wide_cols, 1.5, 0.0)
    mine = full[ds(first, tile, tile), :].astype(jnp.float32)
    mine = (identity - 0.5 * mine).astype(jnp.bfloat16)
    product = times_factor(times_scaled(mine).astype(jnp.bfloat16))
    update = (identity - 0.5 * product).astype(jnp.bfloat16)
    second = times_factor(update).astype(jnp.bfloat16)
    root = jnp.where(table[NEED_AT + block] >= ITERS, second, mine)
    total = jnp.zeros(out.shape[1:], jnp.float32)
    for band in range(bands):
        total = total + jnp.dot(root[:, at(band)], cols[band, 0], preferred_element_type=jnp.float32)
    out[0] = total.astype(jnp.bfloat16)


def newton(table, stat, cols):
    bands, shards, home_count, depth, tile = stat.shape
    width = cols.shape[3]
    return pl.pallas_call(
        newton_kernel,
        out_shape=like((home_count, tile, width)),
        grid_spec=pltpu.PrefetchScalarGridSpec(
            num_scalar_prefetch=1,
            grid=(home_count,),
            in_specs=[
                pl.BlockSpec((bands, shards, 1, depth, tile), lambda i, table: (0, 0, i, 0, 0)),
                pl.BlockSpec((bands, 1, tile, width), lambda i, table: (0, i, 0, 0)),
            ],
            out_specs=pl.BlockSpec((1, tile, width), lambda i, table: (i, 0, 0)),
            scratch_shapes=[pltpu.VMEM((bands * tile, bands * tile), jnp.bfloat16)],
        ),
        compiler_params=BIG,
    )(table, stat, cols)


def exchange(array, axis):
    return lax.all_to_all(array, axis, split_axis=0, concat_axis=0, tiled=True)


def shift(array, step):
    return lax.ppermute(array, REP, [(i, (i + step) % BANDS) for i in range(BANDS)])


def after(array, other):
    return lax.optimization_barrier((array, other))[0]


def tables(owner_map, iterations, home_count):
    levels, turns, shards = lax.axis_size("zl"), lax.axis_size("y"), lax.axis_size(BLK)
    my_level, my_turn, my_blk = lax.axis_index("zl"), lax.axis_index("y"), lax.axis_index(BLK)
    my_own = lax.axis_index(OWN)
    total_blocks = owner_map.shape[0]
    column = turns * home_count
    position = jnp.arange(total_blocks, dtype=jnp.int32)
    same = owner_map[:, None] == owner_map[None, :]
    slot = jnp.sum(jnp.where(same & (position[None, :] < position[:, None]), 1, 0), axis=1)
    place_ids = jnp.arange(levels * turns * shards, dtype=jnp.int32)
    lands = (owner_map * shards + slot)[None, :] == place_ids[:, None]
    holder = jnp.sum(jnp.where(lands, position[None, :] + 1, 0), axis=1) - 1
    holder = holder.reshape(levels, turns, shards)
    mine = holder[my_level, my_turn, my_blk]
    from_ring = (owner_map // turns) * shards + slot
    cut = lax.dynamic_slice_in_dim
    return jnp.concatenate(
        [
            jnp.stack([lax.axis_index(REP), my_blk]),
            cut(owner_map, my_own * home_count, home_count) % turns,
            cut(iterations, my_own * home_count, home_count),
            jnp.maximum(holder, 0)[my_level, my_turn] // column,
            jnp.where(mine >= 0, 1, 0)[None],
            cut(from_ring, my_level * column, column),
            (jnp.maximum(holder, 0) % column)[:, my_turn].reshape(-1),
        ]
    ).astype(jnp.int32)


def body(partial_grads, owner_map, iterations, slot_history):
    turns, shards = lax.axis_size("y"), lax.axis_size(BLK)
    levels = lax.axis_size("zl")
    ring = levels * shards
    my_blk = lax.axis_index(BLK)
    _, home_count, order_full, width = partial_grads.shape
    tile = order_full // BANDS
    size = tile // shards
    depth = STEPS * size
    history = slot_history[0, 0]
    table = tables(owner_map, iterations, home_count)
    place = jnp.stack([lax.axis_index(REP), my_blk]).astype(jnp.int32)

    pairs = lax.axis_size("x")
    half = like((pairs, home_count, tile, width))
    kept, sent = call(fan_kernel, [place, partial_grads[0]], [half, half])
    came = lax.ppermute(sent, "core", [(0, 1), (1, 0)])

    history_there = pltpu.with_memory_space_constraint(history, pltpu.HBM)
    history_parts = exchange(cut_history(place, history_there, tile, shards), BLK)

    chip = call(pair_kernel, [place, kept, came], [like((home_count, tile, width))] * pairs)
    partials = [chip[0]] + [
        lax.ppermute(chip[step], "x", [(i, (i + step) % pairs) for i in range(pairs)])
        for step in range(1, pairs)
    ]
    grad_tile = call(sum_kernel, [place, *partials], like((home_count, tile, width)))

    history_parts = after(history_parts, grad_tile)
    history_sent = jnp.broadcast_to(history_parts[None], (levels,) + history_parts.shape)
    history_level = exchange(history_sent.reshape(ring, depth, tile), "zl")

    grad_cols = lax.all_gather(grad_tile, REP, axis=0, tiled=False)

    grad_band = lax.all_gather(grad_tile, BLK, axis=0, tiled=False)

    history_sent = take(table, after(history_level, grad_band), HISTORY_AT)
    history_sent = history_sent.reshape(turns, home_count, depth, tile)
    history_came = exchange(history_sent, "y")

    mine = lax.dynamic_slice_in_dim(grad_band, my_blk * size, size, 2)
    slices = [shift(mine, -step) for step in range(1, STEPS)]
    gram, gram_sent = call(
        gram_kernel,
        [place, grad_band, *slices],
        [like((home_count, depth, tile), jnp.float32), like((turns, home_count, depth, tile))],
    )
    stat = call(stat_kernel, [table, gram, history_came], like((home_count, depth, tile)))
    stat_band = lax.all_gather(stat, BLK, axis=0, tiled=False)
    gram_came = exchange(gram_sent, "y")
    stat_full = lax.all_gather(after(stat_band, gram_came), REP, axis=0, tiled=False)

    gram_sent = take(table, gram_came.reshape(ring, depth, tile), GRAM_AT)
    gram_level = exchange(gram_sent, "zl")
    gram_slot = call(choose_kernel, [table, gram_level], like((shards, depth, tile)))
    gram_slot = exchange(gram_slot, BLK)
    band, turned = call(
        turn_kernel,
        [table, gram_slot],
        [like((STEPS * tile, tile)), like((BANDS, tile, tile))],
    )
    directions = newton(
        table,
        pltpu.with_memory_space_constraint(stat_full, pltpu.HBM),
        pltpu.with_memory_space_constraint(grad_cols, pltpu.HBM),
    )
    turned = after(exchange(turned, REP), directions)
    new_rows = finish(table, history, band, turned)
    return (directions, new_rows[None, None])


def solution(mesh):
    fine = Mesh(mesh.devices.reshape(4, 2, 4, 8, 4), ("x", "core", "zl", "y", "zh"))
    return jax.shard_map(
        body,
        mesh=fine,
        in_specs=(P(REP, OWN, None, BLK), P(), P(), P(OWN, BLK, None, None)),
        out_specs=(P(OWN, REP, BLK), P(OWN, BLK, REP, None)),
        check_vma=False,
    )
```

```python
import math

import jax
import jax.numpy as jnp
from jax import lax
from jax.experimental import pallas as pl
from jax.experimental.pallas import tpu as pltpu
from jax.sharding import Mesh, PartitionSpec as P

ITERS = 2


DECAY = 0.5
DAMPING = 0.05

REP = ("x", "core")
OWN = ("zl", "y")
BLK = "zh"
RING = ("zl", "zh")

BIG = pltpu.CompilerParams(vmem_limit_bytes=40 * 1024 * 1024)
SCALARS = pl.BlockSpec(memory_space=pltpu.SMEM)
WHOLE = pl.BlockSpec(memory_space=pltpu.VMEM)

BANDS, STEPS = 8, 5
REP_AT, BLK_AT, TURN_AT, NEED_AT, LEVEL_AT, HAS_AT, HISTORY_AT, GRAM_AT = 0, 1, 2, 4, 6, 10, 11, 27


def ds(start, size, unit):
    return pl.ds(pl.multiple_of(start, unit), size)


def like(shape, dtype=jnp.bfloat16):
    return jax.ShapeDtypeStruct(shape, dtype)


def call(kernel, ins, outs, in_specs=None, scratch=()):
    many = isinstance(outs, (list, tuple))
    return pl.pallas_call(
        kernel,
        out_shape=outs,
        in_specs=in_specs or [SCALARS] + [WHOLE] * (len(ins) - 1),
        out_specs=[WHOLE] * len(outs) if many else WHOLE,
        scratch_shapes=list(scratch),
        compiler_params=BIG,
    )(*ins)


def fan_kernel(table, grads, kept, sent):
    pairs, _, rows, _ = kept.shape
    pair, core = lax.div(table[REP_AT], 2), lax.rem(table[REP_AT], 2)
    for step in range(pairs):
        first = lax.rem(pair + step, pairs) * 2
        kept[step] = grads[:, ds((first + core) * rows, rows, rows), :]
        sent[step] = grads[:, ds((first + 1 - core) * rows, rows, rows), :]


def pair_kernel(table, kept, came, *outs):
    for step, out in enumerate(outs):
        total = kept[step].astype(jnp.float32) + came[step].astype(jnp.float32)
        out[...] = total.astype(jnp.bfloat16)


def sum_kernel(table, *refs):
    *ins, out = refs
    total = ins[0][...].astype(jnp.float32)
    for ref in ins[1:]:
        total = total + ref[...].astype(jnp.float32)
    out[...] = total.astype(jnp.bfloat16)


def history_kernel(table, column, out):
    tile = column.shape[1]
    shards = 4
    size = tile // shards
    for step in range(STEPS):
        start = lax.rem(table[REP_AT] + step, BANDS) * tile
        for shard in range(shards):
            piece = column[ds(start + shard * size, size, size), :]
            for level in range(out.shape[0] // shards):
                out[level * shards + shard, step * size : (step + 1) * size] = piece


def cut_history(table, history, places, tile, shards):
    order_full = history.shape[0]
    shape = (places, STEPS * tile // shards, tile)
    return pl.pallas_call(
        history_kernel,
        out_shape=like(shape),
        grid_spec=pltpu.PrefetchScalarGridSpec(
            num_scalar_prefetch=1,
            grid=(1,),
            in_specs=[pl.BlockSpec((order_full, tile), lambda i, table: (0, table[REP_AT]))],
            out_specs=pl.BlockSpec(shape, lambda i, table: (0, 0, 0)),
        ),
        compiler_params=BIG,
    )(table, history)


def take(table, tiles, first):
    def kernel(table, tiles, out):
        for place in range(out.shape[0]):
            out[place] = tiles[table[first + place]]

    return call(kernel, [table, tiles], like(tiles.shape))


def gram_kernel(table, band, *refs):
    *slices, out, sent = refs
    shards, home_count, tile, _ = band.shape
    size = tile // shards
    order_full = BANDS * tile
    start = table[BLK_AT] * size
    for block in range(home_count):
        total = jnp.zeros((STEPS * size, tile), jnp.float32)
        for shard in range(shards):
            left = [band[shard, block, ds(start, size, size), :]]
            left += [ref[shard, block] for ref in slices]
            total = total + lax.dot_general(
                jnp.concatenate(left, axis=0),
                band[shard, block],
                (((1,), (1,)), ((), ())),
                preferred_element_type=jnp.float32,
            )
        total = total * ((1.0 - DECAY) / order_full)
        out[block] = total
        for turn in range(sent.shape[0]):
            sent[turn, block] = total.astype(jnp.bfloat16)


def stat_kernel(table, gram, came, out):
    home_count, depth, tile = out.shape
    size = depth // STEPS
    row_ids = lax.broadcasted_iota(jnp.int32, (depth, tile), 0)
    col_ids = lax.broadcasted_iota(jnp.int32, (depth, tile), 1)
    on = (row_ids < size) & (row_ids + table[BLK_AT] * size == col_ids)
    damping = jnp.where(on, DAMPING, 0.0)
    for block in range(home_count):
        history = came[table[TURN_AT + block], block].astype(jnp.float32)
        out[block] = (DECAY * history + gram[block] + damping).astype(jnp.bfloat16)


def choose_kernel(table, came, out):
    shards = out.shape[0]
    for shard in range(shards):
        out[shard] = came[table[LEVEL_AT + shard] * shards + shard]


def turn_kernel(table, came, band, sent):
    tile = sent.shape[1]
    size = came.shape[1] // STEPS
    shards = tile // size
    for shard in range(shards):
        part = came[shard]
        for step in range(STEPS):
            start = step * tile + shard * size
            band[start : start + size] = part[step * size : (step + 1) * size]
    sent[...] = jnp.zeros_like(sent)
    for step in range(1, STEPS):
        sent[lax.rem(table[REP_AT] + step, BANDS)] = band[step * tile : (step + 1) * tile]


def finish_kernel(table, rows, band, came, out):
    tile = rows.shape[0]
    rep = table[REP_AT]

    def put(column, gram, damping=None):
        columns = ds(column * tile, tile, tile)
        history = rows[:, columns].astype(jnp.float32)
        fresh = DECAY * history + gram
        if damping is not None:
            fresh = fresh + damping
        out[:, columns] = jnp.where(table[HAS_AT] > 0, fresh, history).astype(jnp.bfloat16)

    row_ids = lax.broadcasted_iota(jnp.int32, (tile, tile), 0)
    col_ids = lax.broadcasted_iota(jnp.int32, (tile, tile), 1)
    put(rep, band[:tile].astype(jnp.float32), jnp.where(row_ids == col_ids, DAMPING, 0.0))
    for step in range(1, STEPS):
        other = lax.rem(rep + BANDS - step, BANDS)
        put(other, came[other].astype(jnp.float32))
        if step < STEPS - 1:
            mine = band[step * tile : (step + 1) * tile].astype(jnp.float32)
            put(lax.rem(rep + step, BANDS), mine.T)


def finish(table, history, band, came):
    tile, order_full = band.shape[1], history.shape[1]
    return pl.pallas_call(
        finish_kernel,
        out_shape=like((tile, order_full)),
        grid_spec=pltpu.PrefetchScalarGridSpec(
            num_scalar_prefetch=1,
            grid=(1,),
            in_specs=[
                pl.BlockSpec((tile, order_full), lambda i, table: (table[REP_AT], 0)),
                pl.BlockSpec(band.shape, lambda i, table: (0, 0)),
                pl.BlockSpec(came.shape, lambda i, table: (0, 0, 0)),
            ],
            out_specs=pl.BlockSpec((tile, order_full), lambda i, table: (0, 0)),
        ),
        compiler_params=BIG,
    )(table, history, band, came)


def newton_kernel(table, stat, cols, out, full):
    bands, shards, _, depth, tile = stat.shape
    size = depth // STEPS
    order_full = bands * tile
    block = pl.program_id(0)
    squares = jnp.zeros((8, tile), jnp.float32)
    for band in range(bands):
        for shard in range(shards):
            part = stat[band, shard, 0].astype(jnp.float32)
            part = (part * part).reshape(-1, 8, tile)
            ends, middle = size // 8, (STEPS - 1) * size // 8
            squares = squares + jnp.sum(part, axis=0) + jnp.sum(part[ends:middle], axis=0)
    frobenius = jnp.sqrt(jnp.sum(squares, keepdims=True)[:1, :1])
    norm_scale = math.sqrt(order_full) / (2.0 * frobenius)

    def at(index):
        return slice(index * tile, (index + 1) * tile)

    for band in range(bands):
        for shard in range(shards):
            part = (stat[band, shard, 0].astype(jnp.float32) * norm_scale).astype(jnp.bfloat16)
            for step in range(STEPS):
                start = (band + step) % bands * tile + shard * size
                full[start : start + size, at(band)] = part[step * size : (step + 1) * size]
    for band in range(bands):
        for step in range(1, STEPS - 1):
            other = (band + step) % bands
            full[at(band), at(other)] = full[at(other), at(band)].T

    row_ids = lax.broadcasted_iota(jnp.int32, (tile, tile), 0)
    col_ids = lax.broadcasted_iota(jnp.int32, (tile, tile), 1)
    diagonals = []
    for band in range(bands):
        corner = full[at(band), at(band)].astype(jnp.float32)
        values = jnp.sum(jnp.where(row_ids == col_ids, corner, 0.0), axis=0, keepdims=True)
        rounded = (1.5 - 0.5 * values).astype(jnp.bfloat16).astype(jnp.float32)
        diagonals.append(rounded + 0.5 * values)
    diagonal = jnp.concatenate(diagonals, axis=1)

    def times_scaled(left):
        return jnp.dot(left, full[...], preferred_element_type=jnp.float32)

    def times_factor(left):
        return left.astype(jnp.float32) * diagonal - 0.5 * times_scaled(left)

    first = table[REP_AT] * tile
    wide_rows = lax.broadcasted_iota(jnp.int32, (tile, order_full), 0) + first
    wide_cols = lax.broadcasted_iota(jnp.int32, (tile, order_full), 1)
    identity = jnp.where(wide_rows == wide_cols, 1.5, 0.0)
    mine = full[ds(first, tile, tile), :].astype(jnp.float32)
    mine = (identity - 0.5 * mine).astype(jnp.bfloat16)
    product = times_factor(times_scaled(mine).astype(jnp.bfloat16))
    update = (identity - 0.5 * product).astype(jnp.bfloat16)
    second = times_factor(update).astype(jnp.bfloat16)
    root = jnp.where(table[NEED_AT + block] >= ITERS, second, mine)
    total = jnp.zeros(out.shape[1:], jnp.float32)
    for band in range(bands):
        total = total + jnp.dot(root[:, at(band)], cols[band, 0], preferred_element_type=jnp.float32)
    out[0] = total.astype(jnp.bfloat16)


def newton(table, stat, cols):
    bands, shards, home_count, depth, tile = stat.shape
    width = cols.shape[3]
    return pl.pallas_call(
        newton_kernel,
        out_shape=like((home_count, tile, width)),
        grid_spec=pltpu.PrefetchScalarGridSpec(
            num_scalar_prefetch=1,
            grid=(home_count,),
            in_specs=[
                pl.BlockSpec((bands, shards, 1, depth, tile), lambda i, table: (0, 0, i, 0, 0)),
                pl.BlockSpec((bands, 1, tile, width), lambda i, table: (0, i, 0, 0)),
            ],
            out_specs=pl.BlockSpec((1, tile, width), lambda i, table: (i, 0, 0)),
            scratch_shapes=[pltpu.VMEM((bands * tile, bands * tile), jnp.bfloat16)],
        ),
        compiler_params=BIG,
    )(table, stat, cols)


def exchange(array, axis):
    return lax.all_to_all(array, axis, split_axis=0, concat_axis=0, tiled=True)


def shift(array, step):
    return lax.ppermute(array, REP, [(i, (i + step) % BANDS) for i in range(BANDS)])


def after(array, other):
    return lax.optimization_barrier((array, other))[0]


def tables(owner_map, iterations, home_count):
    levels, turns, shards = lax.axis_size("zl"), lax.axis_size("y"), lax.axis_size(BLK)
    my_level, my_turn, my_blk = lax.axis_index("zl"), lax.axis_index("y"), lax.axis_index(BLK)
    my_own = lax.axis_index(OWN)
    total_blocks = owner_map.shape[0]
    column = turns * home_count
    position = jnp.arange(total_blocks, dtype=jnp.int32)
    same = owner_map[:, None] == owner_map[None, :]
    slot = jnp.sum(jnp.where(same & (position[None, :] < position[:, None]), 1, 0), axis=1)
    place_ids = jnp.arange(levels * turns * shards, dtype=jnp.int32)
    lands = (owner_map * shards + slot)[None, :] == place_ids[:, None]
    holder = jnp.sum(jnp.where(lands, position[None, :] + 1, 0), axis=1) - 1
    holder = holder.reshape(levels, turns, shards)
    mine = holder[my_level, my_turn, my_blk]
    from_ring = (owner_map // turns) * shards + slot
    cut = lax.dynamic_slice_in_dim
    return jnp.concatenate(
        [
            jnp.stack([lax.axis_index(REP), my_blk]),
            cut(owner_map, my_own * home_count, home_count) % turns,
            cut(iterations, my_own * home_count, home_count),
            jnp.maximum(holder, 0)[my_level, my_turn] // column,
            jnp.where(mine >= 0, 1, 0)[None],
            cut(from_ring, my_level * column, column),
            (jnp.maximum(holder, 0) % column)[:, my_turn].reshape(-1),
        ]
    ).astype(jnp.int32)


def body(partial_grads, owner_map, iterations, slot_history):
    turns, shards = lax.axis_size("y"), lax.axis_size(BLK)
    ring = lax.axis_size("zl") * shards
    my_blk = lax.axis_index(BLK)
    _, home_count, order_full, width = partial_grads.shape
    tile = order_full // BANDS
    size = tile // shards
    depth = STEPS * size
    history = slot_history[0, 0]
    history_there = pltpu.with_memory_space_constraint(history, pltpu.HBM)
    table = tables(owner_map, iterations, home_count)
    place = jnp.stack([lax.axis_index(REP), my_blk]).astype(jnp.int32)

    pairs = lax.axis_size("x")
    half = like((pairs, home_count, tile, width))
    kept, sent = call(fan_kernel, [place, partial_grads[0]], [half, half])
    came = lax.ppermute(sent, "core", [(0, 1), (1, 0)])

    history_ring = exchange(cut_history(place, history_there, ring, tile, shards), RING)

    chip = call(pair_kernel, [place, kept, came], [like((home_count, tile, width))] * pairs)
    partials = [chip[0]] + [
        lax.ppermute(chip[step], "x", [(i, (i + step) % pairs) for i in range(pairs)])
        for step in range(1, pairs)
    ]
    grad_tile = call(sum_kernel, [place, *partials], like((home_count, tile, width)))
    grad_cols = lax.all_gather(grad_tile, REP, axis=0, tiled=False)

    grad_band = lax.all_gather(grad_tile, BLK, axis=0, tiled=False)

    history_sent = take(table, after(history_ring, grad_band), HISTORY_AT)
    history_sent = history_sent.reshape(turns, home_count, depth, tile)
    history_came = exchange(history_sent, "y")

    mine = lax.dynamic_slice_in_dim(grad_band, my_blk * size, size, 2)
    slices = [shift(mine, -step) for step in range(1, STEPS)]
    gram, gram_sent = call(
        gram_kernel,
        [place, grad_band, *slices],
        [like((home_count, depth, tile), jnp.float32), like((turns, home_count, depth, tile))],
    )
    stat = call(stat_kernel, [table, gram, history_came], like((home_count, depth, tile)))
    stat_band = lax.all_gather(stat, BLK, axis=0, tiled=False)
    gram_came = exchange(gram_sent, "y")
    stat_full = lax.all_gather(after(stat_band, gram_came), REP, axis=0, tiled=False)

    gram_sent = take(table, gram_came.reshape(ring, depth, tile), GRAM_AT)
    gram_level = exchange(gram_sent, "zl")
    gram_slot = call(choose_kernel, [table, gram_level], like((shards, depth, tile)))
    gram_slot = exchange(gram_slot, BLK)
    band, turned = call(
        turn_kernel,
        [table, gram_slot],
        [like((STEPS * tile, tile)), like((BANDS, tile, tile))],
    )
    directions = newton(
        table,
        pltpu.with_memory_space_constraint(stat_full, pltpu.HBM),
        pltpu.with_memory_space_constraint(grad_cols, pltpu.HBM),
    )
    turned = after(exchange(turned, REP), directions)
    new_rows = finish(table, history, band, turned)
    return (directions, new_rows[None, None])


def solution(mesh):
    fine = Mesh(mesh.devices.reshape(4, 2, 4, 8, 4), ("x", "core", "zl", "y", "zh"))
    return jax.shard_map(
        body,
        mesh=fine,
        in_specs=(P(REP, OWN, None, BLK), P(), P(), P(OWN, BLK, None, None)),
        out_specs=(P(OWN, REP, BLK), P(OWN, BLK, REP, None)),
        check_vma=False,
    )
```
